256 devices in a mesh: prow: 32 (over x, y, core), pcol: 8 (over z).
Axes of the slice: x: 4, y: 4, z: 8, core: 2. Of those that a mesh axis runs over, the one named last changes fastest.
Arguments:
- right_side: float32 [4, 64, 256, 128], P(None, 'prow', 'pcol'), may hold values from -6 to 6
- diag_inverse: float32 [4, 64, 256, 256], P(None, 'prow', None, 'pcol'), as said below
- panels: float32 [3, 64, 8, 256, 256], P(None, 'prow', None, 'pcol'), may hold values from -0.125 to 0.125
- targets: int32 [3, 64, 8], P(None, 'prow'), may hold values from 64 to 255, as said below
Outputs:
- solution: float32 [4, 64, 256, 128], P(None, 'prow', 'pcol')
The draws below stay inside these ranges and needn't reach their ends.
Inputs may be any that keep to these rules, and one draw needn't show every extreme that they name: targets[l, n, k] names a supernode of a level after l: it lies in (l + 1) * 64 to 255; repeats are allowed. diag_inverse is lower triangular with a diagonal in 0.5 to 1.5.
All inputs are finite; a program needn't handle non-finite values.
Results may differ from the reference program's by a relative error of at most 0.0001.
Values sent between devices are 32-bit elements; how exact they have to be, the bound alone decides.
A program may use at most 64 MiB of HBM per device.

```python
import jax
import jax.numpy as jnp
from jax import lax

W = 256
RHS = 128
LEVELS = 4
K_OFF = 8
NS = 64


def draw_diag_inverse(key, part):
    key = jax.random.fold_in(key, 2)
    key_low, key_diag = jax.random.split(key)
    shape = (LEVELS, NS, W, W)
    lower = jax.random.normal(key_low, shape, jnp.float32) * (0.7 / W ** 0.5)
    diag = jax.random.uniform(key_diag, shape, jnp.float32, 0.5, 1.5)
    rows = lax_rows = jnp.arange(W)[:, None]
    cols = jnp.arange(W)[None, :]
    strict = (cols < rows).astype(jnp.float32)
    ident = (cols == lax_rows).astype(jnp.float32)
    return lower * strict + diag * ident


def draw_targets(key, part):
    key = jax.random.fold_in(key, 5)
    shape = (LEVELS - 1, NS, K_OFF)
    level = jnp.arange(LEVELS - 1, dtype=jnp.int32)[:, None, None]
    lowest = (level + 1) * NS
    highest = jnp.full(shape, LEVELS * NS, jnp.int32)
    return jax.random.randint(key, shape, jnp.broadcast_to(lowest, shape), highest).astype(jnp.int32)


def shard_levels(stream_key, extent, cuts, low, top_value):
    level, own = 1.0, jax.random.fold_in(stream_key, 6)
    for dim, parts in cuts:
        heights = jnp.exp(jax.random.uniform(jax.random.fold_in(own, dim), (parts,), jnp.float32, low / len(cuts), top_value / len(cuts)))
        level = level * jnp.repeat(heights, extent[dim] // parts).reshape([-1 if axis == dim else 1 for axis in range(len(extent))])
    return level


def bell_draw(stream_key, shape, deviation, bound, pieces=(), held_as=jnp.bfloat16):
    drawn = deviation * jax.random.normal(stream_key, shape, jnp.float32)
    if pieces:
        drawn = drawn * shard_levels(stream_key, shape, pieces, -0.22, 0.18)
    return jnp.clip(drawn, -bound, bound).astype(held_as)


def setup_inputs(seed: int = 0) -> dict:
    streams_of = jax.random.split(jax.random.key(seed), 5)
    return {
        "right_side": bell_draw(streams_of[0], (LEVELS, NS, W, RHS), 1.0, 6.0, ((1, 32), (2, 8)), jnp.float32),
        "diag_inverse": draw_diag_inverse(jax.random.fold_in(streams_of[4], 71), 0),
        "panels": bell_draw(streams_of[2], (LEVELS - 1, NS, K_OFF, W, W), (W * K_OFF) ** -0.5, 0.125, ((1, 32), (3, 8)), jnp.float32),
        "targets": draw_targets(jax.random.fold_in(streams_of[4], 71), 0),
    }


def reference(right_side, diag_inverse, panels, targets):
    updates = jnp.zeros((LEVELS * NS, W, RHS), jnp.float32)
    solved = []
    for level in range(LEVELS):
        residual = right_side[level] - updates[level * NS:(level + 1) * NS]
        answer = jnp.einsum("nij,njr->nir", diag_inverse[level], residual, precision=lax.Precision.HIGHEST)
        solved.append(answer)
        if level < LEVELS - 1:
            blocks = jnp.einsum("nktj,njr->nktr", panels[level], answer, precision=lax.Precision.HIGHEST)
            places = targets[level].reshape(-1).astype(jnp.int32)
            updates = updates.at[places].add(blocks.reshape(NS * K_OFF, W, RHS))
    return jnp.stack(solved)
```

```python
import functools

import jax
import jax.numpy as jnp
from jax import lax
from jax.experimental import pallas as pl
from jax.experimental.pallas import tpu as pltpu
from jax.sharding import PartitionSpec as P

MESH = pl.DeviceIdType.MESH
LEVELS = 4
STREAMS = 2
CH = 32
LANES = 128
HALF = 64
KB = 8


def dot(a, b):
    return lax.dot_general(
        a, b, (((1,), (0,)), ((), ())),
        precision=lax.Precision.HIGHEST, preferred_element_type=jnp.float32,
    )


def dot_t(a, b):
    return lax.dot_general(
        a, b, (((0,), (0,)), ((), ())),
        precision=lax.Precision.HIGHEST, preferred_element_type=jnp.float32,
    )


def kernel(
    nx, ny, nz,
    rhs_hbm, dinv_hbm, pan_hbm, tgt_hbm, out,
    tgt, rhs_v, dinv_v, pan_v, tbl_v, tbl_s, rp, rs_src, rs_dst, ag, dg, dgt, dbuf, dense, pr, xy, tmp,
    loc, rs_ss, rs_rs, ag_ss, ag_rs, dg_ss, dg_rs, pr_ss, pr_rs, xy_ss, xy_rs,
):
    chips = nx * ny
    width = CH * nz
    count = 4 * chips
    prow = lax.axis_index("prow")
    z = lax.axis_index("pcol")
    core = lax.rem(prow, 2)
    chip = prow // 2
    x = chip // ny
    y = lax.rem(chip, ny)

    def zpeer(k):
        return prow, lax.rem(z + k, nz)

    def xypeer(dx, dy):
        peer = lax.rem(x + dx, nx) * ny + lax.rem(y + dy, ny)
        return peer, (peer * 2 + core, z)

    sibling = (chip * 2 + 1 - core, z)
    offsets = [(dx, dy) for dx in range(nx) for dy in range(ny) if dx or dy]
    offsets.sort(key=lambda o: -(min(o[0], nx - o[0]) + min(o[1], ny - o[1])))
    zorder = sorted(range(1, nz), key=lambda k: -min(k, nz - k))

    def remote(src, dst, ss, rs, dev):
        return pltpu.make_async_remote_copy(
            src_ref=src, dst_ref=dst, send_sem=ss, recv_sem=rs, device_id=dev, device_id_type=MESH
        )

    due, sent = {}, []

    def arrived(*name):
        due.pop(name)()

    def wait_bytes(ref, sem):
        pltpu.make_async_copy(ref, ref, sem).wait()

    c_rhs = pltpu.make_async_copy(rhs_hbm, rhs_v, loc.at[0])
    c_dinv = pltpu.make_async_copy(dinv_hbm, dinv_v, loc.at[1])
    c_tgt = pltpu.make_async_copy(tgt_hbm, tgt, loc.at[6])
    c_tgt.start()
    c_rhs.start()
    c_dinv.start()
    for lev in range(LEVELS - 1):
        c = pltpu.make_async_copy(pan_hbm.at[lev], pan_v.at[lev], loc.at[2 + lev])
        c.start()
        due["pan", lev] = c.wait

    barrier = pltpu.get_barrier_semaphore()
    for k in zorder:
        pl.semaphore_signal(barrier, inc=1, device_id=zpeer(k), device_id_type=MESH)
    for dx, dy in offsets:
        pl.semaphore_signal(barrier, inc=1, device_id=xypeer(dx, dy)[1], device_id_type=MESH)
    pl.semaphore_signal(barrier, inc=1, device_id=sibling, device_id_type=MESH)

    lane = lax.broadcasted_iota(jnp.int32, (1, LANES), 1)
    low = lane < HALF

    c_tgt.wait()
    ids = lax.broadcasted_iota(jnp.int32, (1, LEVELS * count), 1)
    for row in range(2 * (LEVELS - 1)):
        found = jnp.full((1, LEVELS * count), KB, jnp.int32)
        for k in reversed(range(KB)):
            found = jnp.where(ids == tgt[row // 2, row % 2, k], k, found)
        tbl_v[pl.ds(row, 1), :] = found
    c_tbl = pltpu.make_async_copy(tbl_v, tbl_s, loc.at[5])
    c_tbl.start()
    due["tbl",] = c_tbl.wait

    for lev in range(LEVELS - 1):
        for s in range(STREAMS):
            for n in range(2):
                dbuf[lev, s, n, KB] = jnp.zeros((CH, LANES), jnp.float32)
    for i in range(2):
        for s in range(STREAMS):
            for j in range(nz):
                @pl.when(j >= z)
                def _():
                    rs_dst[i, s, j] = jnp.zeros((CH, LANES), jnp.float32)

    c_rhs.wait()
    for lev in range(LEVELS):
        r0, r1 = rhs_v[lev, 0], rhs_v[lev, 1]
        rp[lev, 0] = jnp.where(low, r0, pltpu.roll(r1, HALF, 1))
        rp[lev, 1] = jnp.where(low, pltpu.roll(r0, HALF, 1), r1)
    c_dinv.wait()

    def rs_compute(i, lev, s, res):
        p0 = dot_t(dinv_v[lev, 0], res)
        p1 = dot_t(dinv_v[lev, 1], res)
        rs_src[i, s] = jnp.where(low, p0, p1)

    def rs_arrive(i, s):
        for j in range(nz - 1):
            @pl.when(j < z)
            def _():
                wait_bytes(rs_dst.at[i, s, j], rs_rs.at[i, s, j])

    def rs_left(i, s):
        for k in range(1, nz):
            @pl.when(lax.rem(z + k, nz) > z)
            def _():
                wait_bytes(rs_src.at[i, s, pl.ds(0, CH)], rs_ss.at[i, s, k])

    def rs_send(i, s):
        due["rs", i, s] = lambda: rs_arrive(i, s)
        sent.append(lambda: rs_left(i, s))
        for k in zorder:
            dst = lax.rem(z + k, nz)

            @pl.when(dst > z)
            def _():
                remote(
                    rs_src.at[i, s, pl.ds(dst * CH, CH)], rs_dst.at[i, s, z],
                    rs_ss.at[i, s, k], rs_rs.at[i, s, z], (prow, dst),
                ).start()

    def rs_finish(i, s):
        acc = rs_src[i, s, pl.ds(z * CH, CH)]
        arrived("rs", i, s)
        for j in range(nz - 1):
            acc = acc + rs_dst[i, s, j]
        return acc

    def ag_send(lev, s, val):
        mine = pl.ds(z * CH, CH)
        others = ag.at[lev, s, pl.ds(0, (nz - 1) * CH)]
        due["ag", lev, s] = lambda: wait_bytes(others, ag_rs.at[lev, s])
        sent.append(lambda: wait_bytes(others, ag_ss.at[lev, s]))
        ag[lev, s, mine] = val
        for k in zorder:
            remote(
                ag.at[lev, s, mine], ag.at[lev, s, mine], ag_ss.at[lev, s], ag_rs.at[lev, s], zpeer(k)
            ).start()

    def ag_wait(lev, s):
        arrived("ag", lev, s)
        return ag[lev, s]

    half_steps = nz // 2

    def dg_copies(lev, step):
        d = lev - 1
        up, down = zpeer(1), zpeer(nz - 1)
        cu = lax.rem(z - step + nz, nz)
        cd = lax.rem(z + step, nz)
        res = []
        su = dg.at[d, :, pl.ds(cu * CH, CH)]
        sd = dg.at[d, :, pl.ds(cd * CH, CH)]
        if step < half_steps - 1:
            res.append(remote(su, su, dg_ss.at[d, step, 0], dg_rs.at[d, step, 0], up))
            res.append(remote(sd, sd, dg_ss.at[d, step, 1], dg_rs.at[d, step, 1], down))
        else:
            su = dg.at[d, 0, pl.ds(cu * CH, CH)]
            sd = dg.at[d, 1, pl.ds(cd * CH, CH)]
            res.append(remote(su, su, dg_ss.at[d, step, 0], dg_rs.at[d, step, 0], up))
            res.append(remote(sd, sd, dg_ss.at[d, step, 1], dg_rs.at[d, step, 1], down))
        return res

    def dg_step(lev, step):
        if step >= half_steps:
            return
        if step > 0:
            arrived("dg", lev, step - 1)
        else:
            dg[lev - 1, :, pl.ds(z * CH, CH)] = dinv_v[lev]
        copies = dg_copies(lev, step)
        due["dg", lev, step] = lambda: [c.wait_recv() for c in copies]
        sent.append(lambda: [c.wait_send() for c in copies])
        for c in copies:
            c.start()

    def dg_finish(lev):
        arrived("dg", lev, half_steps - 1)
        for n in range(2):
            dgt[n] = jnp.transpose(dg[lev - 1, n])

    def combine_panels(lev):
        arrived("pan", lev)
        for n in range(2):
            weight = {}
            for a in range(KB):
                for b in range(a + 1, KB):
                    same = tgt[lev, n, a] == tgt[lev, n, b]
                    weight[a, b] = jnp.where(same, 1.0, 0.0)

            def step(i, _, n=n, weight=weight):
                rows = pl.ds(pl.multiple_of(i * 8, 8), 8)
                vals = [pan_v[lev, n, k, rows] for k in range(KB)]
                for a in range(KB):
                    acc = vals[a]
                    for b in range(KB):
                        if b != a:
                            acc = acc + weight[min(a, b), max(a, b)] * vals[b]
                    pan_v[lev, n, a, rows] = acc
                return 0

            lax.fori_loop(0, CH // 8, step, 0)

    def gather(lev, level_to, s, side, b):
        q = core if side == 1 else 1 - core
        t = level_to * count + b * 4 + q * 2
        e0 = dbuf[lev, s, 0, tbl_s[2 * lev, t]] + dbuf[lev, s, 1, tbl_s[2 * lev + 1, t]]
        e1 = dbuf[lev, s, 0, tbl_s[2 * lev, t + 1]] + dbuf[lev, s, 1, tbl_s[2 * lev + 1, t + 1]]
        return jnp.where(low, e0, e1)

    def spread(lev, level_to, s, side):
        def step(b, _):
            val = gather(lev, level_to, s, side, b)
            if lev > 0:
                val = val + dense[level_to - 1, s, side, b]
            dense[level_to - 1, s, side, b] = val
            return 0

        lax.fori_loop(0, chips, step, 0, unroll=4)

    def solve(lev, s):
        r = ag_wait(lev, s)
        if lev > 0:
            a = jnp.where(low, dot(dgt[0], r), dot(dgt[1], r))
        else:
            a = r
        ar = pltpu.roll(a, HALF, 1)
        a0 = jnp.where(low, a, ar)
        a1 = jnp.where(low, ar, a)
        for n, an in ((0, a0), (1, a1)):
            d = dot(pan_v[lev, n].reshape(KB * CH, width), an)
            dbuf[lev, s, n, pl.ds(0, KB)] = d.reshape(KB, CH, LANES)
        spread(lev, lev + 1, s, 0)
        due["pr", lev, s] = lambda: wait_bytes(pr.at[lev, s], pr_rs.at[lev, s])
        sent.append(lambda: wait_bytes(pr.at[lev, s], pr_ss.at[lev, s]))
        remote(dense.at[lev, s, 0], pr.at[lev, s], pr_ss.at[lev, s], pr_rs.at[lev, s], sibling).start()
        tmp[0] = a0
        tmp[1] = a1
        cols = pl.ds(s * HALF, HALF)
        for n in range(2):
            out[lev, n, :, cols] = tmp[n, pl.ds(z * CH, CH), cols]
        spread(lev, lev + 1, s, 1)

    def send_xy(lev, s):
        arrived("pr", lev, s)

        def step(b, _):
            dense[lev, s, 1, b] = dense[lev, s, 1, b] + pr[lev, s, b]
            return 0

        lax.fori_loop(0, chips, step, 0, unroll=4)
        due["xy", lev, s] = lambda: wait_bytes(xy.at[lev, s], xy_rs.at[lev, s])
        sent.append(lambda: wait_bytes(xy.at[lev, s], xy_ss.at[lev, s]))
        for i, (dx, dy) in enumerate(offsets):
            peer, dev = xypeer(dx, dy)
            remote(dense.at[lev, s, 1, peer], xy.at[lev, s, i], xy_ss.at[lev, s], xy_rs.at[lev, s], dev).start()

    def residual(lev, s):
        arrived("xy", lev, s)
        acc = dense[lev, s, 1, chip]
        for i in range(len(offsets)):
            acc = acc + xy[lev, s, i]
        return rp[lev + 1, s] - acc

    for s in range(STREAMS):
        rs_compute(0, 0, s, rp[0, s])

    pl.semaphore_wait(barrier, nz - 1 + len(offsets) + 1)

    both = range(STREAMS)
    for s in both:
        rs_send(0, s)
    dg_step(1, 0)
    combine_panels(0)
    arrived("tbl")
    for s in both:
        ag_send(0, s, rs_finish(0, s))
    dg_step(1, 1)
    for lev in range(LEVELS - 1):
        for s in both:
            solve(lev, s)
        if lev == 0:
            dg_step(1, 2)
        elif lev == 1:
            dg_step(2, 2)
        for s in both:
            send_xy(lev, s)
        if lev == 0:
            dg_step(1, 3)
            dg_step(2, 0)
        elif lev == 1:
            dg_step(2, 3)
        for s in both:
            for to in range(lev + 2, LEVELS):
                for side in range(2):
                    spread(lev, to, s, side)
        if lev + 1 < LEVELS - 1:
            combine_panels(lev + 1)
            dg_finish(lev + 1)
            for s in both:
                ag_send(lev + 1, s, residual(lev, s))
            if lev == 0:
                dg_step(2, 1)
        else:
            for s in both:
                rs_compute(1, LEVELS - 1, s, residual(lev, s))
                rs_send(1, s)
    for s in both:
        a = rs_finish(1, s)
        ar = pltpu.roll(a, HALF, 1)
        cols = pl.ds(s * HALF, HALF)
        tmp[0, pl.ds(0, CH)] = jnp.where(low, a, ar)
        tmp[1, pl.ds(0, CH)] = jnp.where(low, ar, a)
        for n in range(2):
            out[LEVELS - 1, n, :, cols] = tmp[n, pl.ds(0, CH), cols]

    for wait in sent:
        wait()


def shards(nx, ny, nz, right_side, diag_inverse, panels, targets):
    chips = nx * ny
    width = CH * nz
    count = 4 * chips
    f32 = jnp.float32
    dma = pltpu.SemaphoreType.DMA
    hops = nz // 2
    hbm = pl.BlockSpec(memory_space=pltpu.HBM)
    return pl.pallas_call(
        functools.partial(kernel, nx, ny, nz),
        out_shape=jax.ShapeDtypeStruct((LEVELS, 2, CH, LANES), f32),
        in_specs=[hbm] * 4,
        out_specs=pl.BlockSpec(memory_space=pltpu.VMEM),
        scratch_shapes=[
            pltpu.SMEM((LEVELS - 1, 2, KB), jnp.int32),
            pltpu.VMEM((LEVELS, 2, CH, LANES), f32),
            pltpu.VMEM((LEVELS, 2, CH, width), f32),
            pltpu.VMEM((LEVELS - 1, 2, KB, CH, width), f32),
            pltpu.VMEM((8, LEVELS * count), jnp.int32),
            pltpu.SMEM((8, LEVELS * count), jnp.int32),
            pltpu.VMEM((LEVELS, STREAMS, CH, LANES), f32),
            pltpu.VMEM((2, STREAMS, width, LANES), f32),
            pltpu.VMEM((2, STREAMS, nz, CH, LANES), f32),
            pltpu.VMEM((LEVELS - 1, STREAMS, width, LANES), f32),
            pltpu.VMEM((2, 2, width, width), f32),
            pltpu.VMEM((2, width, width), f32),
            pltpu.VMEM((LEVELS - 1, STREAMS, 2, KB + 1, CH, LANES), f32),
            pltpu.VMEM((LEVELS - 1, STREAMS, 2, chips, CH, LANES), f32),
            pltpu.VMEM((LEVELS - 1, STREAMS, chips, CH, LANES), f32),
            pltpu.VMEM((LEVELS - 1, STREAMS, chips - 1, CH, LANES), f32),
            pltpu.VMEM((2, width, LANES), f32),
            dma((7,)),
            dma((2, STREAMS, nz)),
            dma((2, STREAMS, nz)),
            dma((LEVELS - 1, STREAMS)),
            dma((LEVELS - 1, STREAMS)),
            dma((2, hops, 2)),
            dma((2, hops, 2)),
            dma((LEVELS - 1, STREAMS)),
            dma((LEVELS - 1, STREAMS)),
            dma((LEVELS - 1, STREAMS)),
            dma((LEVELS - 1, STREAMS)),
        ],
        compiler_params=pltpu.CompilerParams(
            collective_id=0, has_side_effects=True, vmem_limit_bytes=60 * 1024 * 1024
        ),
    )(right_side, jnp.swapaxes(diag_inverse, 2, 3), panels, targets)


def solution(mesh):
    prow, nz = mesh.shape["prow"], mesh.shape["pcol"]
    ny = 4 if prow == 32 else 1
    nx = prow // (2 * ny)
    in_specs = (
        P(None, "prow", "pcol", None),
        P(None, "prow", None, "pcol"),
        P(None, "prow", None, "pcol", None),
        P(None, "prow", None),
    )
    return jax.shard_map(
        functools.partial(shards, nx, ny, nz), mesh=mesh, in_specs=in_specs,
        out_specs=P(None, "prow", "pcol", None), check_vma=False,
    )
```

```python
import functools

import jax
import jax.numpy as jnp
from jax import lax
from jax.experimental import pallas as pl
from jax.experimental.pallas import tpu as pltpu
from jax.sharding import PartitionSpec as P

MESH = pl.DeviceIdType.MESH
LEVELS = 4
CH = 32
LANES = 128
HALF = 64
KB = 8


def split(a):
    hi = a.astype(jnp.bfloat16)
    return hi, (a - hi.astype(jnp.float32)).astype(jnp.bfloat16)


def dot3(a, b, dims):
    ah, al = split(a)
    bh, bl = split(b)
    f = functools.partial(
        lax.dot_general, dimension_numbers=(dims, ((), ())), preferred_element_type=jnp.float32
    )
    return f(ah, bh) + (f(ah, bl) + f(al, bh))


def dot(a, b):
    return dot3(a, b, ((1,), (0,)))


def dot_t(a, b):
    return dot3(a, b, ((0,), (0,)))


def kernel(
    nx, ny, nz,
    rhs_hbm, dinv_hbm, pan_hbm, tgt_hbm, out,
    tgt, rhs_v, dinv_v, dinv_x, pan_v, tbl_v, tbl_s, rp, rq, rs_src, rs_dst, av, ag, dg, dgt,
    dbuf, dense, xy, tmp, yv, yx,
    loc, rs_ss, rs_rs, ag_ss, ag_rs, dg_ss, dg_rs, xy_ss, xy_rs, sib_ss, sib_rs,
):
    chips = nx * ny
    width = CH * nz
    count = 4 * chips
    prow = lax.axis_index("prow")
    z = lax.axis_index("pcol")
    core = lax.rem(prow, 2)
    chip = prow // 2
    x = chip // ny
    y = lax.rem(chip, ny)
    both = range(2)
    mine = pl.ds(z * CH, CH)

    def zpeer(k):
        return prow, lax.rem(z + k, nz)

    def xypeer(dx, dy):
        peer = lax.rem(x + dx, nx) * ny + lax.rem(y + dy, ny)
        return peer, (peer * 2 + core, z)

    sibling = (chip * 2 + 1 - core, z)
    offsets = [(dx, dy) for dx in range(nx) for dy in range(ny) if dx or dy]
    offsets.sort(key=lambda o: -(min(o[0], nx - o[0]) + min(o[1], ny - o[1])))
    zorder = sorted(range(1, nz), key=lambda k: -min(k, nz - k))

    def remote(src, dst, ss, rs, dev):
        return pltpu.make_async_remote_copy(
            src_ref=src, dst_ref=dst, send_sem=ss, recv_sem=rs, device_id=dev, device_id_type=MESH
        )

    due, sent = {}, []

    def arrived(*name):
        due.pop(name)()

    def wait_bytes(ref, sem):
        pltpu.make_async_copy(ref, ref, sem).wait()

    c_rhs = pltpu.make_async_copy(rhs_hbm, rhs_v, loc.at[0])
    c_dinv = pltpu.make_async_copy(dinv_hbm, dinv_v, loc.at[1])
    c_tgt = pltpu.make_async_copy(tgt_hbm, tgt, loc.at[6])
    c_tgt.start()
    c_rhs.start()
    c_dinv.start()
    for lev in range(LEVELS - 1):
        c = pltpu.make_async_copy(pan_hbm.at[lev], pan_v.at[lev, core], loc.at[2 + lev])
        c.start()
        due["pan", lev] = c.wait

    barrier = pltpu.get_barrier_semaphore()
    for k in zorder:
        for c in both:
            pl.semaphore_signal(
                barrier, inc=1, device_id=(chip * 2 + c, lax.rem(z + k, nz)), device_id_type=MESH
            )
    for dx, dy in offsets:
        pl.semaphore_signal(barrier, inc=1, device_id=xypeer(dx, dy)[1], device_id_type=MESH)
    pl.semaphore_signal(barrier, inc=1, device_id=sibling, device_id_type=MESH)

    lane = lax.broadcasted_iota(jnp.int32, (1, LANES), 1)
    low = lane < HALF

    def sib_send(i, src, dst):
        c = remote(src, dst, sib_ss.at[i], sib_rs.at[i], sibling)
        c.start()
        due["sib", i] = c.wait_recv
        sent.append(c.wait_send)

    c_rhs.wait()
    for lev in range(LEVELS):
        r0, r1 = rhs_v[lev, 0], rhs_v[lev, 1]
        rp[0, lev] = jnp.where(low, r0, pltpu.roll(r1, HALF, 1))
        rp[1, lev] = jnp.where(low, pltpu.roll(r0, HALF, 1), r1)
    c_dinv.wait()
    for s in both:
        r = rp[s, 0]
        rs_src[0, s] = jnp.where(low, dot_t(dinv_v[0, 0], r), dot_t(dinv_v[0, 1], r))

    c_tgt.wait()
    ids = lax.broadcasted_iota(jnp.int32, (1, LEVELS * count), 1)
    for row in range(8):
        found = jnp.full((1, LEVELS * count), KB, jnp.int32)
        if row < 2 * (LEVELS - 1):
            for k in reversed(range(KB)):
                found = jnp.where(ids == tgt[row // 2, row % 2, k], k, found)
        tbl_v[core, pl.ds(row, 1), :] = found

    for lev in range(LEVELS - 1):
        for m in range(4):
            dbuf[lev, m, KB] = jnp.zeros((CH, LANES), jnp.float32)
    for s in both:
        for j in range(nz):
            @pl.when(j >= z)
            def _():
                rs_dst[0, s, j] = jnp.zeros((CH, LANES), jnp.float32)

            @pl.when((j > z) | ((j == z) & (core == s)))
            def _():
                rs_dst[1, s, j] = jnp.zeros((CH, LANES), jnp.float32)

    def rs_send(i, s):
        owner = prow if i == 0 else chip * 2 + s
        slot = s if i == 0 else core

        def arrive():
            for j in range(nz):
                came = j < z
                if i == 1:
                    came = came | ((j == z) & (core != s))

                @pl.when(came)
                def _():
                    wait_bytes(rs_dst.at[i, s, j], rs_rs.at[i, s, j])

        def left():
            for k in range(nz):
                went = lax.rem(z + k, nz) > z if k else core != s
                if k or i == 1:
                    @pl.when(went)
                    def _():
                        wait_bytes(rs_src.at[i, s, pl.ds(0, CH)], rs_ss.at[i, s, k])

        due["rs", i, s] = arrive
        sent.append(left)
        for k in zorder:
            dst = lax.rem(z + k, nz)

            @pl.when(dst > z)
            def _():
                remote(
                    rs_src.at[i, s, pl.ds(dst * CH, CH)], rs_dst.at[i, slot, z],
                    rs_ss.at[i, s, k], rs_rs.at[i, slot, z], (owner, dst),
                ).start()
        if i == 1:
            @pl.when(core != s)
            def _():
                remote(
                    rs_src.at[i, s, mine], rs_dst.at[i, slot, z],
                    rs_ss.at[i, s, 0], rs_rs.at[i, slot, z], sibling,
                ).start()

    def rs_finish(i, s):
        arrived("rs", i, s)
        acc = rs_src[i, s, mine]
        if i == 1:
            acc = jnp.where(core == s, acc, rs_dst[i, s, nz - 1])
        for j in range(nz - 1):
            acc = acc + rs_dst[i, s, j]
        return acc

    def write(lev, x0, x1):
        out[lev, 0] = jnp.where(low, x0, pltpu.roll(x1, HALF, 1))
        out[lev, 1] = jnp.where(low, pltpu.roll(x0, HALF, 1), x1)

    def chunks(lev, p, n):
        return ag.at[lev, p, pl.ds(0, n * CH)]

    def ag_first(s, val):
        def arrive():
            @pl.when(core == s)
            def _():
                wait_bytes(chunks(0, s, nz - 1), ag_rs.at[0, s])

            @pl.when(core != s)
            def _():
                wait_bytes(chunks(0, s, nz), ag_rs.at[0, s])

        def left():
            wait_bytes(chunks(0, s, nz - 1), ag_ss.at[0, s])

            @pl.when(core != s)
            def _():
                wait_bytes(av.at[s], sib_ss.at[AV])

        due["ag", 0, s] = arrive
        sent.append(left)
        av[s] = val
        dst = ag.at[0, core, mine]
        for k in zorder:
            remote(
                av.at[s], dst, ag_ss.at[0, s], ag_rs.at[0, core], (chip * 2 + s, lax.rem(z + k, nz))
            ).start()

        @pl.when(core != s)
        def _():
            remote(av.at[s], dst, sib_ss.at[AV], ag_rs.at[0, core], sibling).start()

        @pl.when(core == s)
        def _():
            ag[0, core, mine] = val

    def ag_send(lev, p, val):
        others = chunks(lev, p, nz - 1)
        due["ag", lev, p] = lambda: wait_bytes(others, ag_rs.at[lev, p])
        sent.append(lambda: wait_bytes(others, ag_ss.at[lev, p]))
        ag[lev, p, mine] = val
        part = ag.at[lev, p, mine]
        for k in zorder:
            remote(part, part, ag_ss.at[lev, p], ag_rs.at[lev, p], zpeer(k)).start()

    half_steps = nz // 2

    def dg_copies(lev, step):
        d = lev - 1
        cu = lax.rem(z - step + nz, nz)
        cd = lax.rem(z + step, nz)
        if step < half_steps - 1:
            su = dg.at[d, :, pl.ds(cu * CH, CH)]
            sd = dg.at[d, :, pl.ds(cd * CH, CH)]
        else:
            su = dg.at[d, 0, pl.ds(cu * CH, CH)]
            sd = dg.at[d, 1, pl.ds(cd * CH, CH)]
        return [
            remote(su, su, dg_ss.at[d, step, 0], dg_rs.at[d, step, 0], zpeer(1)),
            remote(sd, sd, dg_ss.at[d, step, 1], dg_rs.at[d, step, 1], zpeer(nz - 1)),
        ]

    def dg_step(lev, step):
        if step >= half_steps or lev > 2:
            return
        if step > 0:
            arrived("dg", lev, step - 1)
        else:
            dg[lev - 1, :, mine] = dinv_v[lev]
        copies = dg_copies(lev, step)
        due["dg", lev, step] = lambda: [c.wait_recv() for c in copies]
        sent.append(lambda: [c.wait_send() for c in copies])
        for c in copies:
            c.start()

    def dg_finish(lev):
        arrived("dg", lev, half_steps - 1)
        for n in both:
            dgt[lev - 1, core, n] = jnp.transpose(dg[lev - 1, n])
        sib_send(DGT + lev, dgt.at[lev - 1, core], dgt.at[lev - 1, core])

    def combine_panels(lev):
        arrived("pan", lev)
        for n in both:
            weight = {}
            for a in range(KB):
                for b in range(a + 1, KB):
                    same = tgt[lev, n, a] == tgt[lev, n, b]
                    weight[a, b] = jnp.where(same, 1.0, 0.0)

            def step(i, _, n=n, weight=weight):
                rows = pl.ds(pl.multiple_of(i * 8, 8), 8)
                vals = [pan_v[lev, core, n, k, rows] for k in range(KB)]
                for a in range(KB):
                    acc = vals[a]
                    for b in range(KB):
                        if b != a:
                            acc = acc + weight[min(a, b), max(a, b)] * vals[b]
                    pan_v[lev, core, n, a, rows] = acc
                return 0

            lax.fori_loop(0, CH // 8, step, 0)
        sib_send(PAN + lev, pan_v.at[lev, core], pan_v.at[lev, core])

    def gather(lev, level_to, p, b):
        t = level_to * count + b * 4 + p * 2
        e = [None, None]
        for j in both:
            for m in range(4):
                block = dbuf[lev, m, tbl_s[m // 2, 2 * lev + m % 2, t + j]]
                e[j] = block if m == 0 else e[j] + block
        return jnp.where(low, e[0], e[1])

    def spread(lev, level_to, p):
        group = min(chips, 4)

        def step(i, _):
            vals = []
            for j in range(group):
                b = i * group + j
                val = gather(lev, level_to, p, b)
                if lev > 0:
                    val = val + dense[level_to - 1, p, b]
                vals.append(val)
            for j, val in enumerate(vals):
                dense[level_to - 1, p, i * group + j] = val
            return 0

        lax.fori_loop(0, chips // group, step, 0, unroll=True)

    def solve(lev, p):
        arrived("ag", lev, p)
        a = ag[lev, p]
        if lev > 0:
            a = jnp.where(low, dot(dgt[lev - 1, p, 0], a), dot(dgt[lev - 1, p, 1], a))
            tmp[...] = a
            yv[lev - 1, p] = tmp[mine]
        ar = pltpu.roll(a, HALF, 1)
        for n, an in ((0, jnp.where(low, a, ar)), (1, jnp.where(low, ar, a))):
            d = dot(pan_v[lev, p, n].reshape(KB * CH, width), an)
            dbuf[lev, 2 * p + n, pl.ds(0, KB)] = d.reshape(KB, CH, LANES)

    def xy_send(lev, p):
        due["xy", lev, p] = lambda: wait_bytes(xy.at[lev, p], xy_rs.at[lev, p])
        sent.append(lambda: wait_bytes(xy.at[lev, p], xy_ss.at[lev, p]))
        for i, (dx, dy) in enumerate(offsets):
            peer, dev = xypeer(dx, dy)
            remote(dense.at[lev, p, peer], xy.at[lev, p, i], xy_ss.at[lev, p], xy_rs.at[lev, p], dev).start()

    def residual(lev, p):
        arrived("xy", lev, p)
        acc = dense[lev, p, chip]
        for i in range(len(offsets)):
            acc = acc + xy[lev, p, i]
        return rq[p, lev] - acc

    pl.semaphore_wait(barrier, 2 * (nz - 1) + len(offsets) + 1)

    for s in both:
        rs_send(0, s)
    sib_send(TBL, tbl_v.at[core], tbl_v.at[core])
    sib_send(RHS, rp.at[1 - core, pl.ds(1, LEVELS - 1)], rq.at[core])
    sib_send(INV, dinv_v.at[LEVELS - 1], dinv_x.at[core])
    rq[core] = rp[core, pl.ds(1, LEVELS - 1)]
    dinv_x[core] = dinv_v[LEVELS - 1]
    dg_step(1, 0)
    combine_panels(0)
    first = []
    for s in both:
        val = rs_finish(0, s)
        ag_first(s, val)
        first.append(val)
    dg_step(1, 1)
    write(0, *first)
    arrived("sib", TBL)
    c_tbl = pltpu.make_async_copy(tbl_v, tbl_s, loc.at[5])
    c_tbl.start()
    combine_panels(1)
    combine_panels(2)
    c_tbl.wait()
    arrived("sib", RHS)
    arrived("sib", INV)
    for lev in range(LEVELS - 1):
        arrived("sib", PAN + lev)
        if lev > 0:
            arrived("sib", DGT + lev)
        solve(lev, 0)
        dg_step(lev + 1, 2)
        solve(lev, 1)
        for p in both:
            spread(lev, lev + 1, p)
            xy_send(lev, p)
        dg_step(lev + 1, 3)
        dg_step(lev + 2, 0)
        if lev > 0:
            sib_send(ANS + lev, yv.at[lev - 1, 1 - core], yx.at[lev - 1])
        for to in range(lev + 2, LEVELS):
            for p in both:
                spread(lev, to, p)
        if lev < LEVELS - 2:
            dg_finish(lev + 1)
            for p in both:
                ag_send(lev + 1, p, residual(lev, p))
            dg_step(lev + 2, 1)
        else:
            for p in both:
                r = residual(lev, p)
                rs_src[1, p] = jnp.where(low, dot_t(dinv_x[p, 0], r), dot_t(dinv_x[p, 1], r))
                rs_send(1, p)
    for lev in (1, 2):
        arrived("sib", ANS + lev)
        own, other = yv[lev - 1, core], yx[lev - 1]
        write(lev, jnp.where(core == 0, own, other), jnp.where(core == 0, other, own))
    write(LEVELS - 1, rs_finish(1, 0), rs_finish(1, 1))

    for wait in sent:
        wait()


TBL, RHS, INV, AV, PAN, DGT, ANS, SIBS = 0, 1, 2, 3, 4, 6, 8, 11


def shards(nx, ny, nz, right_side, diag_inverse, panels, targets):
    chips = nx * ny
    width = CH * nz
    count = 4 * chips
    f32 = jnp.float32
    dma = pltpu.SemaphoreType.DMA
    vmem = pltpu.VMEM
    hops = nz // 2
    solved = LEVELS - 1
    hbm = pl.BlockSpec(memory_space=pltpu.HBM)
    return pl.pallas_call(
        functools.partial(kernel, nx, ny, nz),
        out_shape=jax.ShapeDtypeStruct((LEVELS, 2, CH, LANES), f32),
        in_specs=[hbm] * 4,
        out_specs=pl.BlockSpec(memory_space=pltpu.VMEM),
        scratch_shapes=[
            pltpu.SMEM((solved, 2, KB), jnp.int32),
            vmem((LEVELS, 2, CH, LANES), f32),
            vmem((LEVELS, 2, CH, width), f32),
            vmem((2, 2, CH, width), f32),
            vmem((solved, 2, 2, KB, CH, width), f32),
            vmem((2, 8, LEVELS * count), jnp.int32),
            pltpu.SMEM((2, 8, LEVELS * count), jnp.int32),
            vmem((2, LEVELS, CH, LANES), f32),
            vmem((2, solved, CH, LANES), f32),
            vmem((2, 2, width, LANES), f32),
            vmem((2, 2, nz, CH, LANES), f32),
            vmem((2, CH, LANES), f32),
            vmem((solved, 2, width, LANES), f32),
            vmem((2, 2, width, width), f32),
            vmem((2, 2, 2, width, width), f32),
            vmem((solved, 4, KB + 1, CH, LANES), f32),
            vmem((solved, 2, chips, CH, LANES), f32),
            vmem((solved, 2, chips - 1, CH, LANES), f32),
            vmem((width, LANES), f32),
            vmem((2, 2, CH, LANES), f32),
            vmem((2, CH, LANES), f32),
            dma((7,)),
            dma((2, 2, nz)),
            dma((2, 2, nz)),
            dma((solved, 2)),
            dma((solved, 2)),
            dma((2, hops, 2)),
            dma((2, hops, 2)),
            dma((solved, 2)),
            dma((solved, 2)),
            dma((SIBS,)),
            dma((SIBS,)),
        ],
        compiler_params=pltpu.CompilerParams(
            collective_id=0, has_side_effects=True, vmem_limit_bytes=60 * 1024 * 1024
        ),
    )(right_side, jnp.swapaxes(diag_inverse, 2, 3), panels, targets)


def solution(mesh):
    prow, nz = mesh.shape["prow"], mesh.shape["pcol"]
    ny = 4 if prow == 32 else 1
    nx = prow // (2 * ny)
    in_specs = (
        P(None, "prow", "pcol", None),
        P(None, "prow", None, "pcol"),
        P(None, "prow", None, "pcol", None),
        P(None, "prow", None),
    )
    return jax.shard_map(
        functools.partial(shards, nx, ny, nz), mesh=mesh, in_specs=in_specs,
        out_specs=P(None, "prow", "pcol", None), check_vma=False,
    )
```

```python
import functools

import jax
import jax.numpy as jnp
from jax import lax
from jax.experimental import pallas as pl
from jax.experimental.pallas import tpu as pltpu
from jax.sharding import PartitionSpec as P

MESH = pl.DeviceIdType.MESH
LEVELS = 4
CH = 32
LANES = 128
HALF = 64
KB = 8


def split(a):
    hi = a.astype(jnp.bfloat16)
    return hi, (a - hi.astype(jnp.float32)).astype(jnp.bfloat16)


def dot3(a, b, dims):
    ah, al = split(a)
    bh, bl = split(b)
    f = functools.partial(
        lax.dot_general, dimension_numbers=(dims, ((), ())), preferred_element_type=jnp.float32
    )
    n = b.shape[1]
    wide = f(ah, jnp.concatenate([bh, bl], axis=1))
    return wide[:, :n] + (wide[:, n:] + f(al, bh))


def dot(a, b):
    return dot3(a, b, ((1,), (0,)))


def dot_t(a, b):
    return dot3(a, b, ((0,), (0,)))


def kernel(
    nx, ny, nz,
    rhs_hbm, dinv_hbm, pan_hbm, tgt_hbm, out,
    tgt, rhs_v, dinv_v, dinv_x, pan_v, tbl_v, tbl_s, rp, rqp, rq, rs_src, rs_dst, fs_src, fs_dst, av, ag, dg, dgt,
    dbuf, dense, xy, tmp, yv, yo, yx,
    loc, rs_ss, rs_rs, fs_ss, fs_rs, ag_ss, ag_rs, dg_ss, dg_rs, xy_ss, xy_rs, sib_ss, sib_rs,
):
    chips = nx * ny
    width = CH * nz
    count = 4 * chips
    prow = lax.axis_index("prow")
    z = lax.axis_index("pcol")
    core = lax.rem(prow, 2)
    chip = prow // 2
    x = chip // ny
    y = lax.rem(chip, ny)
    both = range(2)
    mine = pl.ds(z * CH, CH)

    def zpeer(k):
        return prow, lax.rem(z + k, nz)

    def xypeer(dx, dy):
        peer = lax.rem(x + dx, nx) * ny + lax.rem(y + dy, ny)
        return peer, (peer * 2 + core, z)

    sibling = (chip * 2 + 1 - core, z)
    offsets = [(dx, dy) for dx in range(nx) for dy in range(ny) if dx or dy]
    offsets.sort(key=lambda o: -(min(o[0], nx - o[0]) + min(o[1], ny - o[1])))
    zorder = sorted(range(1, nz), key=lambda k: -min(k, nz - k))

    def remote(src, dst, ss, rs, dev):
        return pltpu.make_async_remote_copy(
            src_ref=src, dst_ref=dst, send_sem=ss, recv_sem=rs, device_id=dev, device_id_type=MESH
        )

    due, sent = {}, []

    def arrived(*name):
        due.pop(name)()

    def wait_bytes(ref, sem):
        pltpu.make_async_copy(ref, ref, sem).wait()

    c_rhs = pltpu.make_async_copy(rhs_hbm, rhs_v, loc.at[0])
    c_dinv = pltpu.make_async_copy(dinv_hbm, dinv_v, loc.at[1])
    c_tgt = pltpu.make_async_copy(tgt_hbm, tgt, loc.at[6])
    c_tgt.start()
    c_rhs.start()
    c_dinv.start()
    for lev in range(LEVELS - 1):
        c = pltpu.make_async_copy(pan_hbm.at[lev], pan_v.at[lev, core], loc.at[2 + lev])
        c.start()
        due["pan", lev] = c.wait

    barrier = pltpu.get_barrier_semaphore()
    for k in zorder:
        for c in both:
            pl.semaphore_signal(
                barrier, inc=1, device_id=(chip * 2 + c, lax.rem(z + k, nz)), device_id_type=MESH
            )
    for dx, dy in offsets:
        pl.semaphore_signal(barrier, inc=1, device_id=xypeer(dx, dy)[1], device_id_type=MESH)
    pl.semaphore_signal(barrier, inc=1, device_id=sibling, device_id_type=MESH)

    lane = lax.broadcasted_iota(jnp.int32, (1, LANES), 1)
    low = lane < HALF
    first_q, third_q = lane < HALF // 2, lane < HALF // 2 * 3

    def quarters(a, b, c, d):
        return jnp.where(low, jnp.where(first_q, a, b), jnp.where(third_q, c, d))

    def turn(v, k):
        return pltpu.roll(v, k % 4 * (HALF // 2), 1) if k % 4 else v

    def to_streams(v, w):
        return (
            quarters(v, turn(v, -1), turn(w, 2), turn(w, 1)),
            quarters(turn(v, -1), turn(v, -2), turn(w, 1), w),
        )

    def to_packs(v, w):
        return (
            quarters(v, turn(w, 1), turn(v, 1), turn(w, 2)),
            quarters(turn(v, -2), turn(w, -1), turn(v, -1), w),
        )

    def sib_send(i, src, dst):
        c = remote(src, dst, sib_ss.at[i], sib_rs.at[i], sibling)
        c.start()
        due["sib", i] = c.wait_recv
        sent.append(c.wait_send)

    c_rhs.wait()
    for lev in range(LEVELS):
        r0, r1 = rhs_v[lev, 0], rhs_v[lev, 1]
        rp[0, lev] = jnp.where(low, r0, pltpu.roll(r1, HALF, 1))
        rp[1, lev] = jnp.where(low, pltpu.roll(r0, HALF, 1), r1)
    c_dinv.wait()
    for s in both:
        r = rp[s, 0]
        rs_src[s] = jnp.where(low, dot_t(dinv_v[0, 0], r), dot_t(dinv_v[0, 1], r))

    c_tgt.wait()
    ids = lax.broadcasted_iota(jnp.int32, (1, LEVELS * count), 1)
    for row in range(8):
        found = jnp.full((1, LEVELS * count), KB, jnp.int32)
        if row < 2 * (LEVELS - 1):
            for k in reversed(range(KB)):
                found = jnp.where(ids == tgt[row // 2, row % 2, k], k, found)
        tbl_v[core, pl.ds(row, 1), :] = found

    for lev in range(LEVELS - 1):
        for u in both:
            for m in range(4):
                dbuf[lev, u, m, KB] = jnp.zeros((CH, LANES), jnp.float32)
    for s in both:
        for j in range(nz):
            @pl.when(j >= z)
            def _():
                rs_dst[s, j] = jnp.zeros((CH, LANES), jnp.float32)

            @pl.when((j > z) | ((j == z) & (core == s)))
            def _():
                for u in both:
                    fs_dst[u, s, j] = jnp.zeros((CH // 2, LANES), jnp.float32)

    def rs_send(s):
        def arrive():
            for j in range(nz - 1):
                @pl.when(j < z)
                def _():
                    wait_bytes(rs_dst.at[s, j], rs_rs.at[s, j])

        def left():
            for k in range(1, nz):
                @pl.when(lax.rem(z + k, nz) > z)
                def _():
                    wait_bytes(rs_src.at[s, pl.ds(0, CH)], rs_ss.at[s, k])

        due["rs", s] = arrive
        sent.append(left)
        for k in zorder:
            dst = lax.rem(z + k, nz)

            @pl.when(dst > z)
            def _():
                remote(
                    rs_src.at[s, pl.ds(dst * CH, CH)], rs_dst.at[s, z],
                    rs_ss.at[s, k], rs_rs.at[s, z], (prow, dst),
                ).start()

    def rs_finish(s):
        arrived("rs", s)
        acc = rs_src[s, mine]
        for j in range(nz - 1):
            acc = acc + rs_dst[s, j]
        return acc

    def fs_send(u, r):
        p = quarters(*[dot_t(dinv_x[m // 2, m % 2], r) for m in range(4)])
        for b in range(nz):
            top, bottom = p[b * CH : b * CH + CH // 2], p[b * CH + CH // 2 : (b + 1) * CH]
            fs_src[u, 0, b] = jnp.where(low, top, turn(bottom, 2))
            fs_src[u, 1, b] = jnp.where(low, turn(top, 2), bottom)

        def arrive():
            for h in both:
                for j in range(nz):
                    @pl.when((j < z) | ((j == z) & (core != h)))
                    def _():
                        wait_bytes(fs_dst.at[u, h, j], fs_rs.at[u, h, j])

        def left():
            for q in both:
                for k in range(nz):
                    @pl.when(lax.rem(z + k, nz) > z if k else core != q)
                    def _():
                        wait_bytes(fs_src.at[u, q, 0], fs_ss.at[u, q, k])

        due["fs", u] = arrive
        sent.append(left)
        for k in zorder + [0]:
            dst = lax.rem(z + k, nz)
            for q in both:
                @pl.when(dst > z if k else core != q)
                def _():
                    remote(
                        fs_src.at[u, q, dst], fs_dst.at[u, core, z],
                        fs_ss.at[u, q, k], fs_rs.at[u, core, z], (chip * 2 + q, dst),
                    ).start()

    def fs_finish(u):
        arrived("fs", u)
        res = []
        for h in both:
            acc = jnp.where(core == h, fs_src[u, h, z], fs_dst[u, h, nz - 1])
            for j in range(nz - 1):
                acc = acc + fs_dst[u, h, j]
            res.append(jnp.concatenate([acc, turn(acc, 2)], axis=0))
        return res

    def write(lev, x0, x1):
        out[lev, 0] = jnp.where(low, x0, pltpu.roll(x1, HALF, 1))
        out[lev, 1] = jnp.where(low, pltpu.roll(x0, HALF, 1), x1)

    def chunks(lev, p, n):
        return ag.at[lev, p, pl.ds(0, n * CH)]

    def ag_first(s, val):
        def arrive():
            @pl.when(core == s)
            def _():
                wait_bytes(chunks(0, s, nz - 1), ag_rs.at[0, s])

            @pl.when(core != s)
            def _():
                wait_bytes(chunks(0, s, nz), ag_rs.at[0, s])

        def left():
            wait_bytes(chunks(0, s, nz - 1), ag_ss.at[0, s])

            @pl.when(core != s)
            def _():
                wait_bytes(av.at[s], sib_ss.at[AV])

        due["ag", 0, s] = arrive
        sent.append(left)
        av[s] = val
        dst = ag.at[0, core, mine]
        for k in zorder:
            remote(
                av.at[s], dst, ag_ss.at[0, s], ag_rs.at[0, core], (chip * 2 + s, lax.rem(z + k, nz))
            ).start()

        @pl.when(core != s)
        def _():
            remote(av.at[s], dst, sib_ss.at[AV], ag_rs.at[0, core], sibling).start()

        @pl.when(core == s)
        def _():
            ag[0, core, mine] = val

    def ag_send(lev, p, val):
        others = chunks(lev, p, nz - 1)
        due["ag", lev, p] = lambda: wait_bytes(others, ag_rs.at[lev, p])
        sent.append(lambda: wait_bytes(others, ag_ss.at[lev, p]))
        ag[lev, p, mine] = val
        part = ag.at[lev, p, mine]
        for k in zorder:
            remote(part, part, ag_ss.at[lev, p], ag_rs.at[lev, p], zpeer(k)).start()

    relays = {
        8: [
            [(0, 1, None), (0, -1, None)],
            [(-1, 1, None), (1, -1, None)],
            [(-2, 2, 0), (2, -2, 1), (-2, 1, None), (2, -1, None)],
        ],
        4: [[(0, 1, None), (0, -1, None)], [(-1, 1, 0), (1, -1, 1)]],
    }[nz]

    def dg_copies(lev, step):
        d = lev - 1
        res = []
        for i, (off, far, n) in enumerate(relays[step]):
            rows = pl.ds(lax.rem(z + off + nz, nz) * CH, CH)
            part = dg.at[d, :, rows] if n is None else dg.at[d, n, rows]
            res.append(remote(part, part, dg_ss.at[d, step, i], dg_rs.at[d, step, i], zpeer(far + nz)))
        return res

    def dg_step(lev, step):
        if step >= len(relays) or lev > 2:
            return
        if step > 0:
            arrived("dg", lev, step - 1)
        else:
            dg[lev - 1, :, mine] = dinv_v[lev]
        copies = dg_copies(lev, step)
        due["dg", lev, step] = lambda: [c.wait_recv() for c in copies]
        sent.append(lambda: [c.wait_send() for c in copies])
        for c in copies:
            c.start()

    def dg_finish(lev):
        arrived("dg", lev, len(relays) - 1)
        for n in both:
            dgt[lev - 1, core, n] = jnp.transpose(dg[lev - 1, n])
        sib_send(DGT + lev, dgt.at[lev - 1, core], dgt.at[lev - 1, core])

    def combine_panels(lev):
        arrived("pan", lev)
        for n in both:
            weight = {}
            for a in range(KB):
                for b in range(a + 1, KB):
                    same = tgt[lev, n, a] == tgt[lev, n, b]
                    weight[a, b] = jnp.where(same, 1.0, 0.0)

            def step(i, _, n=n, weight=weight):
                rows = pl.ds(pl.multiple_of(i * 8, 8), 8)
                vals = [pan_v[lev, core, n, k, rows] for k in range(KB)]
                for a in range(KB):
                    acc = vals[a]
                    for b in range(KB):
                        if b != a:
                            acc = acc + weight[min(a, b), max(a, b)] * vals[b]
                    pan_v[lev, core, n, a, rows] = acc
                return 0

            lax.fori_loop(0, CH // 8, step, 0)
        sib_send(PAN + lev, pan_v.at[lev, core], pan_v.at[lev, core])

    def gather(lev, level_to, u, b):
        t = level_to * count + b * 4
        e = []
        for j in range(4):
            acc = None
            for m in range(4):
                block = dbuf[lev, u, m, tbl_s[m // 2, 2 * lev + m % 2, t + j]]
                acc = block if m == 0 else acc + block
            e.append(acc)
        return quarters(*e)

    def spread(lev, level_to, p):
        group = min(chips, 4)

        def step(i, _):
            vals = []
            for j in range(group):
                b = i * group + j
                val = gather(lev, level_to, p, b)
                if lev > 0:
                    val = val + dense[level_to - 1, p, b]
                vals.append(val)
            for j, val in enumerate(vals):
                dense[level_to - 1, p, i * group + j] = val
            return 0

        lax.fori_loop(0, chips // group, step, 0, unroll=True)

    def solve(lev, u, a):
        if lev > 0:
            arrived("ag", lev, u)
            r = ag[lev, u]
            a = quarters(*[dot(dgt[lev - 1, m // 2, m % 2], r) for m in range(4)])
            tmp[...] = a
            yv[lev - 1, u] = tmp[mine]
        turned = [turn(a, k) for k in range(4)]
        for m in range(4):
            am = quarters(*[turned[(j - m) % 4] for j in range(4)])
            d = dot(pan_v[lev, m // 2, m % 2].reshape(KB * CH, width), am)
            dbuf[lev, u, m, pl.ds(0, KB)] = d.reshape(KB, CH, LANES)

    def xy_send(lev, p):
        due["xy", lev, p] = lambda: wait_bytes(xy.at[lev, p], xy_rs.at[lev, p])
        sent.append(lambda: wait_bytes(xy.at[lev, p], xy_ss.at[lev, p]))
        for i, (dx, dy) in enumerate(offsets):
            peer, dev = xypeer(dx, dy)
            remote(dense.at[lev, p, peer], xy.at[lev, p, i], xy_ss.at[lev, p], xy_rs.at[lev, p], dev).start()

    def residual(lev, p):
        arrived("xy", lev, p)
        acc = dense[lev, p, chip]
        for i in range(len(offsets)):
            acc = acc + xy[lev, p, i]
        return rq[p, lev] - acc

    pl.semaphore_wait(barrier, 2 * (nz - 1) + len(offsets) + 1)

    for s in both:
        rs_send(s)
    sib_send(TBL, tbl_v.at[core], tbl_v.at[core])
    sib_send(RHS, rp.at[1 - core, pl.ds(1, LEVELS - 1)], rqp.at[core])
    sib_send(INV, dinv_v.at[LEVELS - 1], dinv_x.at[core])
    rqp[core] = rp[core, pl.ds(1, LEVELS - 1)]
    dinv_x[core] = dinv_v[LEVELS - 1]
    dg_step(1, 0)
    combine_panels(0)
    first = []
    for s in both:
        val = rs_finish(s)
        ag_first(s, val)
        first.append(val)
    dg_step(1, 1)
    write(0, *first)
    arrived("sib", TBL)
    c_tbl = pltpu.make_async_copy(tbl_v, tbl_s, loc.at[5])
    c_tbl.start()
    due["tbl",] = c_tbl.wait
    combine_panels(1)
    combine_panels(2)
    arrived("tbl")
    arrived("sib", RHS)
    arrived("sib", INV)
    for lev in range(LEVELS - 1):
        rq[0, lev], rq[1, lev] = to_streams(rqp[0, lev], rqp[1, lev])
    for lev in range(LEVELS - 1):
        arrived("sib", PAN + lev)
        if lev > 0:
            arrived("sib", DGT + lev)
        if lev == 0:
            arrived("ag", 0, 0)
            arrived("ag", 0, 1)
            start = to_streams(ag[0, 0], ag[0, 1])
        for u in both:
            solve(lev, u, start[u])
            spread(lev, lev + 1, u)
            xy_send(lev, u)
        dg_step(lev + 1, 2)
        dg_step(lev + 2, 0)
        if lev > 0:
            packs = to_packs(yv[lev - 1, 0], yv[lev - 1, 1])
            yo[lev - 1, 0] = jnp.where(core == 0, packs[0], packs[1])
            yo[lev - 1, 1] = jnp.where(core == 0, packs[1], packs[0])
            sib_send(ANS + lev, yo.at[lev - 1, 1], yx.at[lev - 1])
        for to in range(lev + 2, LEVELS):
            for p in both:
                spread(lev, to, p)
        if lev < LEVELS - 2:
            for p in both:
                ag_send(lev + 1, p, residual(lev, p))
            dg_finish(lev + 1)
            dg_step(lev + 2, 1)
        else:
            for p in both:
                fs_send(p, residual(lev, p))
    for lev in (1, 2):
        arrived("sib", ANS + lev)
        own, other = yo[lev - 1, 0], yx[lev - 1]
        write(lev, jnp.where(core == 0, own, other), jnp.where(core == 0, other, own))
    last = [fs_finish(0), fs_finish(1)]
    write(LEVELS - 1, *[
        quarters(last[0][h], turn(last[1][h], 1), turn(last[0][h], 1), turn(last[1][h], 2)) for h in both
    ])

    for wait in sent:
        wait()


TBL, RHS, INV, AV, PAN, DGT, ANS, SIBS = 0, 1, 2, 3, 4, 6, 8, 11


def shards(nx, ny, nz, right_side, diag_inverse, panels, targets):
    chips = nx * ny
    width = CH * nz
    count = 4 * chips
    f32 = jnp.float32
    dma = pltpu.SemaphoreType.DMA
    vmem = pltpu.VMEM
    solved = LEVELS - 1
    hbm = pl.BlockSpec(memory_space=pltpu.HBM)
    return pl.pallas_call(
        functools.partial(kernel, nx, ny, nz),
        out_shape=jax.ShapeDtypeStruct((LEVELS, 2, CH, LANES), f32),
        in_specs=[hbm] * 4,
        out_specs=pl.BlockSpec(memory_space=pltpu.VMEM),
        scratch_shapes=[
            pltpu.SMEM((solved, 2, KB), jnp.int32),
            vmem((LEVELS, 2, CH, LANES), f32),
            vmem((LEVELS, 2, CH, width), f32),
            vmem((2, 2, CH, width), f32),
            vmem((solved, 2, 2, KB, CH, width), f32),
            vmem((2, 8, LEVELS * count), jnp.int32),
            pltpu.SMEM((2, 8, LEVELS * count), jnp.int32),
            vmem((2, LEVELS, CH, LANES), f32),
            vmem((2, solved, CH, LANES), f32),
            vmem((2, solved, CH, LANES), f32),
            vmem((2, width, LANES), f32),
            vmem((2, nz, CH, LANES), f32),
            vmem((2, 2, nz, CH // 2, LANES), f32),
            vmem((2, 2, nz, CH // 2, LANES), f32),
            vmem((2, CH, LANES), f32),
            vmem((solved, 2, width, LANES), f32),
            vmem((2, 2, width, width), f32),
            vmem((2, 2, 2, width, width), f32),
            vmem((solved, 2, 4, KB + 1, CH, LANES), f32),
            vmem((solved, 2, chips, CH, LANES), f32),
            vmem((solved, 2, chips - 1, CH, LANES), f32),
            vmem((width, LANES), f32),
            vmem((2, 2, CH, LANES), f32),
            vmem((2, 2, CH, LANES), f32),
            vmem((2, CH, LANES), f32),
            dma((7,)),
            dma((2, nz)),
            dma((2, nz)),
            dma((2, 2, nz)),
            dma((2, 2, nz)),
            dma((solved, 2)),
            dma((solved, 2)),
            dma((2, 3, 4)),
            dma((2, 3, 4)),
            dma((solved, 2)),
            dma((solved, 2)),
            dma((SIBS,)),
            dma((SIBS,)),
        ],
        compiler_params=pltpu.CompilerParams(
            collective_id=0, has_side_effects=True, vmem_limit_bytes=60 * 1024 * 1024
        ),
    )(right_side, jnp.swapaxes(diag_inverse, 2, 3), panels, targets)


def solution(mesh):
    prow, nz = mesh.shape["prow"], mesh.shape["pcol"]
    ny = 4 if prow == 32 else 1
    nx = prow // (2 * ny)
    in_specs = (
        P(None, "prow", "pcol", None),
        P(None, "prow", None, "pcol"),
        P(None, "prow", None, "pcol", None),
        P(None, "prow", None),
    )
    return jax.shard_map(
        functools.partial(shards, nx, ny, nz), mesh=mesh, in_specs=in_specs,
        out_specs=P(None, "prow", "pcol", None), check_vma=False,
    )
```

```python
import functools

import jax
import jax.numpy as jnp
from jax import lax
from jax.experimental import pallas as pl
from jax.experimental.pallas import tpu as pltpu
from jax.sharding import PartitionSpec as P

MESH = pl.DeviceIdType.MESH
LEVELS = 4
CH = 32
LANES = 128
HALF = 64
KB = 8


def split(a):
    hi = a.astype(jnp.bfloat16)
    return hi, (a - hi.astype(jnp.float32)).astype(jnp.bfloat16)


def dot3(ah, al, b, dims=((1,), (0,))):
    bh, bl = split(b)
    f = functools.partial(
        lax.dot_general, dimension_numbers=(dims, ((), ())), preferred_element_type=jnp.float32
    )
    n = b.shape[1]
    wide = f(ah, jnp.concatenate([bh, bl], axis=1))
    return wide[:, :n] + (wide[:, n:] + f(al, bh))


def dot_t(a, b):
    return dot3(*split(a), b, ((0,), (0,)))


def kernel(
    nx, ny, nz,
    rhs_hbm, dinv_hbm, pan_hbm, tgt_hbm, out,
    tgt, rhs_v, dinv_v, dinv_x, pan_v, tbl_v, tbl_s, rp, rqp, rq, rs_src, rs_dst, fs_src, fs_dst, av, ag, dg, dgt,
    dbuf, dense, xy, tmp, yv, yo, yx, ps, ds,
    loc, rs_ss, rs_rs, fs_ss, fs_rs, ag_ss, ag_rs, dg_ss, dg_rs, xy_ss, xy_rs, sib_ss, sib_rs,
):
    chips = nx * ny
    width = CH * nz
    count = 4 * chips
    prow = lax.axis_index("prow")
    z = lax.axis_index("pcol")
    core = lax.rem(prow, 2)
    chip = prow // 2
    x = chip // ny
    y = lax.rem(chip, ny)
    both = range(2)
    mine = pl.ds(z * CH, CH)

    def zpeer(k):
        return prow, lax.rem(z + k, nz)

    def xypeer(dx, dy):
        peer = lax.rem(x + dx, nx) * ny + lax.rem(y + dy, ny)
        return peer, (peer * 2 + core, z)

    sibling = (chip * 2 + 1 - core, z)
    offsets = [(dx, dy) for dx in range(nx) for dy in range(ny) if dx or dy]
    offsets.sort(key=lambda o: -(min(o[0], nx - o[0]) + min(o[1], ny - o[1])))
    zorder = sorted(range(1, nz), key=lambda k: -min(k, nz - k))

    def remote(src, dst, ss, rs, dev):
        return pltpu.make_async_remote_copy(
            src_ref=src, dst_ref=dst, send_sem=ss, recv_sem=rs, device_id=dev, device_id_type=MESH
        )

    due, sent = {}, []

    def arrived(*name):
        due.pop(name)()

    def wait_bytes(ref, sem):
        pltpu.make_async_copy(ref, ref, sem).wait()

    c_rhs = pltpu.make_async_copy(rhs_hbm, rhs_v, loc.at[0])
    c_dinv = pltpu.make_async_copy(dinv_hbm, dinv_v, loc.at[1])
    c_tgt = pltpu.make_async_copy(tgt_hbm, tgt, loc.at[6])
    c_tgt.start()
    c_rhs.start()
    c_dinv.start()
    for lev in range(LEVELS - 1):
        c = pltpu.make_async_copy(pan_hbm.at[lev], pan_v.at[lev, core], loc.at[2 + lev])
        c.start()
        due["pan", lev] = c.wait

    barrier = pltpu.get_barrier_semaphore()
    for k in zorder:
        for c in both:
            pl.semaphore_signal(
                barrier, inc=1, device_id=(chip * 2 + c, lax.rem(z + k, nz)), device_id_type=MESH
            )
    for dx, dy in offsets:
        pl.semaphore_signal(barrier, inc=1, device_id=xypeer(dx, dy)[1], device_id_type=MESH)
    pl.semaphore_signal(barrier, inc=1, device_id=sibling, device_id_type=MESH)

    lane = lax.broadcasted_iota(jnp.int32, (1, LANES), 1)
    low = lane < HALF
    first_q, third_q = lane < HALF // 2, lane < HALF // 2 * 3

    def quarters(a, b, c, d):
        return jnp.where(low, jnp.where(first_q, a, b), jnp.where(third_q, c, d))

    def turn(v, k):
        return pltpu.roll(v, k % 4 * (HALF // 2), 1) if k % 4 else v

    def to_streams(v, w):
        return (
            quarters(v, turn(v, -1), turn(w, 2), turn(w, 1)),
            quarters(turn(v, -1), turn(v, -2), turn(w, 1), w),
        )

    def to_packs(v, w):
        return (
            quarters(v, turn(w, 1), turn(v, 1), turn(w, 2)),
            quarters(turn(v, -2), turn(w, -1), turn(v, -1), w),
        )

    def sib_send(i, src, dst):
        c = remote(src, dst, sib_ss.at[i], sib_rs.at[i], sibling)
        c.start()
        due["sib", i] = c.wait_recv
        sent.append(c.wait_send)

    c_rhs.wait()
    for lev in range(LEVELS):
        r0, r1 = rhs_v[lev, 0], rhs_v[lev, 1]
        rp[0, lev] = jnp.where(low, r0, pltpu.roll(r1, HALF, 1))
        rp[1, lev] = jnp.where(low, pltpu.roll(r0, HALF, 1), r1)
    c_dinv.wait()
    for s in both:
        r = rp[s, 0]
        rs_src[s] = jnp.where(low, dot_t(dinv_v[0, 0], r), dot_t(dinv_v[0, 1], r))

    c_tgt.wait()
    ids = lax.broadcasted_iota(jnp.int32, (1, LEVELS * count), 1)
    for row in range(8):
        found = jnp.full((1, LEVELS * count), KB, jnp.int32)
        if row < 2 * (LEVELS - 1):
            for k in reversed(range(KB)):
                found = jnp.where(ids == tgt[row // 2, row % 2, k], k, found)
        tbl_v[core, pl.ds(row, 1), :] = found

    for lev in range(LEVELS - 1):
        for u in both:
            for m in range(4):
                dbuf[lev, u, m, KB] = jnp.zeros((CH, LANES), jnp.float32)
    for s in both:
        for j in range(nz):
            @pl.when(j >= z)
            def _():
                rs_dst[s, j] = jnp.zeros((CH, LANES), jnp.float32)

            @pl.when((j > z) | ((j == z) & (core == s)))
            def _():
                for u in both:
                    fs_dst[u, s, j] = jnp.zeros((CH // 2, LANES), jnp.float32)

    def rs_send(s):
        def arrive():
            for j in range(nz - 1):
                @pl.when(j < z)
                def _():
                    wait_bytes(rs_dst.at[s, j], rs_rs.at[s, j])

        def left():
            for k in range(1, nz):
                @pl.when(lax.rem(z + k, nz) > z)
                def _():
                    wait_bytes(rs_src.at[s, pl.ds(0, CH)], rs_ss.at[s, k])

        due["rs", s] = arrive
        sent.append(left)
        for k in zorder:
            dst = lax.rem(z + k, nz)

            @pl.when(dst > z)
            def _():
                remote(
                    rs_src.at[s, pl.ds(dst * CH, CH)], rs_dst.at[s, z],
                    rs_ss.at[s, k], rs_rs.at[s, z], (prow, dst),
                ).start()

    def rs_finish(s):
        arrived("rs", s)
        acc = rs_src[s, mine]
        for j in range(nz - 1):
            acc = acc + rs_dst[s, j]
        return acc

    def fs_send(u, r):
        p = quarters(*[dot_t(dinv_x[m // 2, m % 2], r) for m in range(4)])
        for b in range(nz):
            top, bottom = p[b * CH : b * CH + CH // 2], p[b * CH + CH // 2 : (b + 1) * CH]
            fs_src[u, 0, b] = jnp.where(low, top, turn(bottom, 2))
            fs_src[u, 1, b] = jnp.where(low, turn(top, 2), bottom)

        def arrive():
            for h in both:
                for j in range(nz):
                    @pl.when((j < z) | ((j == z) & (core != h)))
                    def _():
                        wait_bytes(fs_dst.at[u, h, j], fs_rs.at[u, h, j])

        def left():
            for q in both:
                for k in range(nz):
                    @pl.when(lax.rem(z + k, nz) > z if k else core != q)
                    def _():
                        wait_bytes(fs_src.at[u, q, 0], fs_ss.at[u, q, k])

        due["fs", u] = arrive
        sent.append(left)
        for k in zorder + [0]:
            dst = lax.rem(z + k, nz)
            for q in both:
                @pl.when(dst > z if k else core != q)
                def _():
                    remote(
                        fs_src.at[u, q, dst], fs_dst.at[u, core, z],
                        fs_ss.at[u, q, k], fs_rs.at[u, core, z], (chip * 2 + q, dst),
                    ).start()

    def fs_finish(u):
        arrived("fs", u)
        res = []
        for h in both:
            acc = jnp.where(core == h, fs_src[u, h, z], fs_dst[u, h, nz - 1])
            for j in range(nz - 1):
                acc = acc + fs_dst[u, h, j]
            res.append(jnp.concatenate([acc, turn(acc, 2)], axis=0))
        return res

    def write(lev, x0, x1):
        out[lev, 0] = jnp.where(low, x0, pltpu.roll(x1, HALF, 1))
        out[lev, 1] = jnp.where(low, pltpu.roll(x0, HALF, 1), x1)

    def chunks(lev, p, n):
        return ag.at[lev, p, pl.ds(0, n * CH)]

    def ag_first(s, val):
        def arrive():
            @pl.when(core == s)
            def _():
                wait_bytes(chunks(0, s, nz - 1), ag_rs.at[0, s])

            @pl.when(core != s)
            def _():
                wait_bytes(chunks(0, s, nz), ag_rs.at[0, s])

        def left():
            wait_bytes(chunks(0, s, nz - 1), ag_ss.at[0, s])

            @pl.when(core != s)
            def _():
                wait_bytes(av.at[s], sib_ss.at[AV])

        due["ag", 0, s] = arrive
        sent.append(left)
        av[s] = val
        dst = ag.at[0, core, mine]
        for k in zorder:
            remote(
                av.at[s], dst, ag_ss.at[0, s], ag_rs.at[0, core], (chip * 2 + s, lax.rem(z + k, nz))
            ).start()

        @pl.when(core != s)
        def _():
            remote(av.at[s], dst, sib_ss.at[AV], ag_rs.at[0, core], sibling).start()

        @pl.when(core == s)
        def _():
            ag[0, core, mine] = val

    def ag_send(lev, p, val):
        others = chunks(lev, p, nz - 1)
        due["ag", lev, p] = lambda: wait_bytes(others, ag_rs.at[lev, p])
        sent.append(lambda: wait_bytes(others, ag_ss.at[lev, p]))
        ag[lev, p, mine] = val
        part = ag.at[lev, p, mine]
        for k in zorder:
            remote(part, part, ag_ss.at[lev, p], ag_rs.at[lev, p], zpeer(k)).start()

    relays = {
        8: [
            [(0, 1, None), (0, -1, None)],
            [(-1, 1, None), (1, -1, None)],
            [(-2, 2, 0), (2, -2, 1), (-2, 1, None), (2, -1, None)],
        ],
        4: [[(0, 1, None), (0, -1, None)], [(-1, 1, 0), (1, -1, 1)]],
    }[nz]

    def dg_copies(lev, step):
        d = lev - 1
        res = []
        for i, (off, far, n) in enumerate(relays[step]):
            rows = pl.ds(lax.rem(z + off + nz, nz) * CH, CH)
            part = dg.at[d, :, rows] if n is None else dg.at[d, n, rows]
            res.append(remote(part, part, dg_ss.at[d, step, i], dg_rs.at[d, step, i], zpeer(far + nz)))
        return res

    def dg_step(lev, step):
        if step >= len(relays) or lev > 2:
            return
        if step > 0:
            arrived("dg", lev, step - 1)
        else:
            dg[lev - 1, :, mine] = dinv_v[lev]
        copies = dg_copies(lev, step)
        due["dg", lev, step] = lambda: [c.wait_recv() for c in copies]
        sent.append(lambda: [c.wait_send() for c in copies])
        for c in copies:
            c.start()

    def dg_finish(lev):
        arrived("dg", lev, len(relays) - 1)
        for n in both:
            dgt[lev - 1, core, n] = jnp.transpose(dg[lev - 1, n])
        sib_send(DGT + lev, dgt.at[lev - 1, core], dgt.at[lev - 1, core])

    def combine_panels(lev):
        arrived("pan", lev)
        for n in both:
            weight = {}
            for a in range(KB):
                for b in range(a + 1, KB):
                    same = tgt[lev, n, a] == tgt[lev, n, b]
                    weight[a, b] = jnp.where(same, 1.0, 0.0)

            def step(i, _, n=n, weight=weight):
                rows = pl.ds(pl.multiple_of(i * 8, 8), 8)
                vals = [pan_v[lev, core, n, k, rows] for k in range(KB)]
                for a in range(KB):
                    acc = vals[a]
                    for b in range(KB):
                        if b != a:
                            acc = acc + weight[min(a, b), max(a, b)] * vals[b]
                    pan_v[lev, core, n, a, rows] = acc
                return 0

            lax.fori_loop(0, CH // 8, step, 0)
        sib_send(PAN + lev, pan_v.at[lev, core], pan_v.at[lev, core])

    def gather(lev, level_to, u, b):
        t = level_to * count + b * 4
        e = []
        for j in range(4):
            acc = None
            for m in range(4):
                block = dbuf[lev, u, m, tbl_s[m // 2, 2 * lev + m % 2, t + j]]
                acc = block if m == 0 else acc + block
            e.append(acc)
        return quarters(*e)

    def spread(lev, level_to, p):
        group = min(chips, 4)

        def step(i, _):
            vals = []
            for j in range(group):
                b = i * group + j
                val = gather(lev, level_to, p, b)
                if lev > 0:
                    val = val + dense[level_to - 1, p, b]
                vals.append(val)
            for j, val in enumerate(vals):
                dense[level_to - 1, p, i * group + j] = val
            return 0

        lax.fori_loop(0, chips // group, step, 0, unroll=True)

    def split_panels(lev):
        arrived("sib", PAN + lev)
        for m in range(4):
            ps[lev, m, 0], ps[lev, m, 1] = split(pan_v[lev, m // 2, m % 2].reshape(KB * CH, width))

    def split_inverse(lev):
        arrived("sib", DGT + lev)
        for m in range(4):
            ds[m, 0], ds[m, 1] = split(dgt[lev - 1, m // 2, m % 2])

    def solve(lev, u):
        if lev > 0:
            wait_bytes(chunks(lev, u, nz - 1), ag_rs.at[lev, u])
        r = a = ag[lev, u]
        if lev > 0:
            a = quarters(*[dot3(ds[m, 0], ds[m, 1], r) for m in range(4)])
            tmp[...] = a
            yv[lev - 1, u] = tmp[mine]
        turned = [turn(a, k) for k in range(4)]
        for m in range(4):
            am = quarters(*[turned[(j - m) % 4] for j in range(4)])
            d = dot3(ps[lev, m, 0], ps[lev, m, 1], am)
            dbuf[lev, u, m, pl.ds(0, KB)] = d.reshape(KB, CH, LANES)

    def spread_send(lev, u):
        places = [(i, *xypeer(dx, dy)) for i, (dx, dy) in enumerate(offsets)]
        places.append((None, chip, None))
        for g in range(0, len(places), 4):
            group = places[g : g + 4]
            vals = []
            for _, b, _ in group:
                val = gather(lev, lev + 1, u, b)
                vals.append(val + dense[lev, u, b] if lev > 0 else val)
            for (_, b, _), val in zip(group, vals):
                dense[lev, u, b] = val
            for i, b, dev in group:
                if i is not None:
                    remote(
                        dense.at[lev, u, b], xy.at[lev, u, i], xy_ss.at[lev, u], xy_rs.at[lev, u], dev
                    ).start()

    def residual(lev, p):
        arrived("xy", lev, p)
        acc = dense[lev, p, chip]
        for i in range(len(offsets)):
            acc = acc + xy[lev, p, i]
        return rq[p, lev] - acc

    pl.semaphore_wait(barrier, 2 * (nz - 1) + len(offsets) + 1)

    for s in both:
        rs_send(s)
    sib_send(TBL, tbl_v.at[core], tbl_v.at[core])
    sib_send(RHS, rp.at[1 - core, pl.ds(1, LEVELS - 1)], rqp.at[core])
    sib_send(INV, dinv_v.at[LEVELS - 1], dinv_x.at[core])
    rqp[core] = rp[core, pl.ds(1, LEVELS - 1)]
    dinv_x[core] = dinv_v[LEVELS - 1]
    dg_step(1, 0)
    combine_panels(0)
    first = []
    for s in both:
        val = rs_finish(s)
        ag_first(s, val)
        first.append(val)
    dg_step(1, 1)
    write(0, *first)
    arrived("sib", TBL)
    c_tbl = pltpu.make_async_copy(tbl_v, tbl_s, loc.at[5])
    c_tbl.start()
    due["tbl",] = c_tbl.wait
    combine_panels(1)
    combine_panels(2)
    arrived("tbl")
    split_panels(0)
    arrived("sib", RHS)
    arrived("sib", INV)
    for lev in range(LEVELS - 1):
        rq[0, lev], rq[1, lev] = to_streams(rqp[0, lev], rqp[1, lev])
    for lev in range(LEVELS - 1):
        if lev == 0:
            arrived("ag", 0, 0)
            arrived("ag", 0, 1)
            ag[0, 0], ag[0, 1] = to_streams(ag[0, 0], ag[0, 1])

        def work(u, _, lev=lev):
            solve(lev, u)
            spread_send(lev, u)
            return 0

        lax.fori_loop(0, 2, work, 0)
        for u in both:
            due.pop(("ag", lev, u), None)
            due["xy", lev, u] = lambda lev=lev, u=u: wait_bytes(xy.at[lev, u], xy_rs.at[lev, u])
            sent.append(lambda lev=lev, u=u: wait_bytes(xy.at[lev, u], xy_ss.at[lev, u]))
        dg_step(lev + 1, 2)
        dg_step(lev + 2, 0)
        if lev > 0:
            packs = to_packs(yv[lev - 1, 0], yv[lev - 1, 1])
            yo[lev - 1, 0] = jnp.where(core == 0, packs[0], packs[1])
            yo[lev - 1, 1] = jnp.where(core == 0, packs[1], packs[0])
            sib_send(ANS + lev, yo.at[lev - 1, 1], yx.at[lev - 1])
        for to in range(lev + 2, LEVELS):
            def later(u, _, lev=lev, to=to):
                spread(lev, to, u)
                return 0

            lax.fori_loop(0, 2, later, 0)
        if lev < LEVELS - 2:
            split_panels(lev + 1)
            for p in both:
                ag_send(lev + 1, p, residual(lev, p))
            dg_finish(lev + 1)
            dg_step(lev + 2, 1)
            split_inverse(lev + 1)
        else:
            for p in both:
                fs_send(p, residual(lev, p))
    for lev in (1, 2):
        arrived("sib", ANS + lev)
        own, other = yo[lev - 1, 0], yx[lev - 1]
        write(lev, jnp.where(core == 0, own, other), jnp.where(core == 0, other, own))
    last = [fs_finish(0), fs_finish(1)]
    write(LEVELS - 1, *[
        quarters(last[0][h], turn(last[1][h], 1), turn(last[0][h], 1), turn(last[1][h], 2)) for h in both
    ])

    for wait in sent:
        wait()


TBL, RHS, INV, AV, PAN, DGT, ANS, SIBS = 0, 1, 2, 3, 4, 6, 8, 11


def shards(nx, ny, nz, right_side, diag_inverse, panels, targets):
    chips = nx * ny
    width = CH * nz
    count = 4 * chips
    f32 = jnp.float32
    dma = pltpu.SemaphoreType.DMA
    vmem = pltpu.VMEM
    solved = LEVELS - 1
    hbm = pl.BlockSpec(memory_space=pltpu.HBM)
    return pl.pallas_call(
        functools.partial(kernel, nx, ny, nz),
        out_shape=jax.ShapeDtypeStruct((LEVELS, 2, CH, LANES), f32),
        in_specs=[hbm] * 4,
        out_specs=pl.BlockSpec(memory_space=pltpu.VMEM),
        scratch_shapes=[
            pltpu.SMEM((solved, 2, KB), jnp.int32),
            vmem((LEVELS, 2, CH, LANES), f32),
            vmem((LEVELS, 2, CH, width), f32),
            vmem((2, 2, CH, width), f32),
            vmem((solved, 2, 2, KB, CH, width), f32),
            vmem((2, 8, LEVELS * count), jnp.int32),
            pltpu.SMEM((2, 8, LEVELS * count), jnp.int32),
            vmem((2, LEVELS, CH, LANES), f32),
            vmem((2, solved, CH, LANES), f32),
            vmem((2, solved, CH, LANES), f32),
            vmem((2, width, LANES), f32),
            vmem((2, nz, CH, LANES), f32),
            vmem((2, 2, nz, CH // 2, LANES), f32),
            vmem((2, 2, nz, CH // 2, LANES), f32),
            vmem((2, CH, LANES), f32),
            vmem((solved, 2, width, LANES), f32),
            vmem((2, 2, width, width), f32),
            vmem((2, 2, 2, width, width), f32),
            vmem((solved, 2, 4, KB + 1, CH, LANES), f32),
            vmem((solved, 2, chips, CH, LANES), f32),
            vmem((solved, 2, chips - 1, CH, LANES), f32),
            vmem((width, LANES), f32),
            vmem((2, 2, CH, LANES), f32),
            vmem((2, 2, CH, LANES), f32),
            vmem((2, CH, LANES), f32),
            vmem((solved, 4, 2, KB * CH, width), jnp.bfloat16),
            vmem((4, 2, width, width), jnp.bfloat16),
            dma((7,)),
            dma((2, nz)),
            dma((2, nz)),
            dma((2, 2, nz)),
            dma((2, 2, nz)),
            dma((solved, 2)),
            dma((solved, 2)),
            dma((2, 3, 4)),
            dma((2, 3, 4)),
            dma((solved, 2)),
            dma((solved, 2)),
            dma((SIBS,)),
            dma((SIBS,)),
        ],
        compiler_params=pltpu.CompilerParams(
            collective_id=0, has_side_effects=True, vmem_limit_bytes=60 * 1024 * 1024
        ),
    )(right_side, jnp.swapaxes(diag_inverse, 2, 3), panels, targets)


def solution(mesh):
    prow, nz = mesh.shape["prow"], mesh.shape["pcol"]
    ny = 4 if prow == 32 else 1
    nx = prow // (2 * ny)
    in_specs = (
        P(None, "prow", "pcol", None),
        P(None, "prow", None, "pcol"),
        P(None, "prow", None, "pcol", None),
        P(None, "prow", None),
    )
    return jax.shard_map(
        functools.partial(shards, nx, ny, nz), mesh=mesh, in_specs=in_specs,
        out_specs=P(None, "prow", "pcol", None), check_vma=False,
    )
```

```python
import functools

import jax
import jax.numpy as jnp
from jax import lax
from jax.experimental import pallas as pl
from jax.experimental.pallas import tpu as pltpu
from jax.sharding import PartitionSpec as P

MESH = pl.DeviceIdType.MESH
LEVELS = 4
CH = 32
LANES = 128
HALF = 64
KB = 8


def split(a):
    hi = a.astype(jnp.bfloat16)
    return hi, (a - hi.astype(jnp.float32)).astype(jnp.bfloat16)


def dot3(a, b, dims):
    ah, al = split(a)
    bh, bl = split(b)
    f = functools.partial(
        lax.dot_general, dimension_numbers=(dims, ((), ())), preferred_element_type=jnp.float32
    )
    n = b.shape[1]
    wide = f(ah, jnp.concatenate([bh, bl], axis=1))
    return wide[:, :n] + (wide[:, n:] + f(al, bh))


def dot(a, b):
    return dot3(a, b, ((1,), (0,)))


def dot_t(a, b):
    return dot3(a, b, ((0,), (0,)))


def kernel(
    nx, ny, nz,
    rhs_hbm, dinv_hbm, pan_hbm, tgt_hbm, out,
    tgt, rhs_v, dinv_v, dinv_x, pan_v, tbl_v, tbl_s, rp, rqp, rq, rs_src, rs_dst, fs_src, fs_dst, av, ag, dg, dgt,
    dbuf, dense, xy, tmp, yv, yo, yx,
    loc, rs_ss, rs_rs, fs_ss, fs_rs, ag_ss, ag_rs, dg_ss, dg_rs, xy_ss, xy_rs, sib_ss, sib_rs,
):
    chips = nx * ny
    width = CH * nz
    count = 4 * chips
    prow = lax.axis_index("prow")
    z = lax.axis_index("pcol")
    core = lax.rem(prow, 2)
    chip = prow // 2
    x = chip // ny
    y = lax.rem(chip, ny)
    both = range(2)
    mine = pl.ds(z * CH, CH)

    def zpeer(k):
        return prow, lax.rem(z + k, nz)

    def xypeer(dx, dy):
        peer = lax.rem(x + dx, nx) * ny + lax.rem(y + dy, ny)
        return peer, (peer * 2 + core, z)

    sibling = (chip * 2 + 1 - core, z)
    offsets = [(dx, dy) for dx in range(nx) for dy in range(ny) if dx or dy]
    offsets.sort(key=lambda o: -(min(o[0], nx - o[0]) + min(o[1], ny - o[1])))
    zorder = sorted(range(1, nz), key=lambda k: -min(k, nz - k))

    def remote(src, dst, ss, rs, dev):
        return pltpu.make_async_remote_copy(
            src_ref=src, dst_ref=dst, send_sem=ss, recv_sem=rs, device_id=dev, device_id_type=MESH
        )

    due, sent = {}, []

    def arrived(*name):
        due.pop(name)()

    def wait_bytes(ref, sem):
        pltpu.make_async_copy(ref, ref, sem).wait()

    c_rhs = pltpu.make_async_copy(rhs_hbm, rhs_v, loc.at[0])
    c_dinv = pltpu.make_async_copy(dinv_hbm, dinv_v, loc.at[1])
    c_tgt = pltpu.make_async_copy(tgt_hbm, tgt, loc.at[6])
    c_tgt.start()
    c_rhs.start()
    c_dinv.start()
    for lev in range(LEVELS - 1):
        c = pltpu.make_async_copy(pan_hbm.at[lev], pan_v.at[lev, core], loc.at[2 + lev])
        c.start()
        due["pan", lev] = c.wait

    barrier = pltpu.get_barrier_semaphore()
    for k in zorder:
        for c in both:
            pl.semaphore_signal(
                barrier, inc=1, device_id=(chip * 2 + c, lax.rem(z + k, nz)), device_id_type=MESH
            )
    for dx, dy in offsets:
        pl.semaphore_signal(barrier, inc=1, device_id=xypeer(dx, dy)[1], device_id_type=MESH)
    pl.semaphore_signal(barrier, inc=1, device_id=sibling, device_id_type=MESH)

    lane = lax.broadcasted_iota(jnp.int32, (1, LANES), 1)
    low = lane < HALF
    first_q, third_q = lane < HALF // 2, lane < HALF // 2 * 3

    def quarters(a, b, c, d):
        return jnp.where(low, jnp.where(first_q, a, b), jnp.where(third_q, c, d))

    def turn(v, k):
        return pltpu.roll(v, k % 4 * (HALF // 2), 1) if k % 4 else v

    def to_streams(v, w):
        return (
            quarters(v, turn(v, -1), turn(w, 2), turn(w, 1)),
            quarters(turn(v, -1), turn(v, -2), turn(w, 1), w),
        )

    def to_packs(v, w):
        return (
            quarters(v, turn(w, 1), turn(v, 1), turn(w, 2)),
            quarters(turn(v, -2), turn(w, -1), turn(v, -1), w),
        )

    def sib_send(i, src, dst):
        c = remote(src, dst, sib_ss.at[i], sib_rs.at[i], sibling)
        c.start()
        due["sib", i] = c.wait_recv
        sent.append(c.wait_send)

    c_rhs.wait()
    for lev in range(LEVELS):
        r0, r1 = rhs_v[lev, 0], rhs_v[lev, 1]
        rp[0, lev] = jnp.where(low, r0, pltpu.roll(r1, HALF, 1))
        rp[1, lev] = jnp.where(low, pltpu.roll(r0, HALF, 1), r1)
    c_dinv.wait()
    for s in both:
        r = rp[s, 0]
        rs_src[s] = jnp.where(low, dot_t(dinv_v[0, 0], r), dot_t(dinv_v[0, 1], r))

    c_tgt.wait()
    ids = lax.broadcasted_iota(jnp.int32, (1, LEVELS * count), 1)
    for row in range(8):
        found = jnp.full((1, LEVELS * count), KB, jnp.int32)
        if row < 2 * (LEVELS - 1):
            for k in reversed(range(KB)):
                found = jnp.where(ids == tgt[row // 2, row % 2, k], k, found)
        tbl_v[core, pl.ds(row, 1), :] = found

    for lev in range(LEVELS - 1):
        for u in both:
            for m in range(4):
                dbuf[lev, u, m, KB] = jnp.zeros((CH, LANES), jnp.float32)
    for s in both:
        for j in range(nz):
            @pl.when(j >= z)
            def _():
                rs_dst[s, j] = jnp.zeros((CH, LANES), jnp.float32)

            @pl.when((j > z) | ((j == z) & (core == s)))
            def _():
                for u in both:
                    fs_dst[u, s, j] = jnp.zeros((CH // 2, LANES), jnp.float32)

    def rs_send(s):
        def arrive():
            for j in range(nz - 1):
                @pl.when(j < z)
                def _():
                    wait_bytes(rs_dst.at[s, j], rs_rs.at[s, j])

        def left():
            for k in range(1, nz):
                @pl.when(lax.rem(z + k, nz) > z)
                def _():
                    wait_bytes(rs_src.at[s, pl.ds(0, CH)], rs_ss.at[s, k])

        due["rs", s] = arrive
        sent.append(left)
        for k in zorder:
            dst = lax.rem(z + k, nz)

            @pl.when(dst > z)
            def _():
                remote(
                    rs_src.at[s, pl.ds(dst * CH, CH)], rs_dst.at[s, z],
                    rs_ss.at[s, k], rs_rs.at[s, z], (prow, dst),
                ).start()

    def rs_finish(s):
        arrived("rs", s)
        acc = rs_src[s, mine]
        for j in range(nz - 1):
            acc = acc + rs_dst[s, j]
        return acc

    def fs_send(u, r):
        p = quarters(*[dot_t(dinv_x[m // 2, m % 2], r) for m in range(4)])
        for b in range(nz):
            top, bottom = p[b * CH : b * CH + CH // 2], p[b * CH + CH // 2 : (b + 1) * CH]
            fs_src[u, 0, b] = jnp.where(low, top, turn(bottom, 2))
            fs_src[u, 1, b] = jnp.where(low, turn(top, 2), bottom)

        def arrive():
            for h in both:
                for j in range(nz):
                    @pl.when((j < z) | ((j == z) & (core != h)))
                    def _():
                        wait_bytes(fs_dst.at[u, h, j], fs_rs.at[u, h, j])

        def left():
            for q in both:
                for k in range(nz):
                    @pl.when(lax.rem(z + k, nz) > z if k else core != q)
                    def _():
                        wait_bytes(fs_src.at[u, q, 0], fs_ss.at[u, q, k])

        due["fs", u] = arrive
        sent.append(left)
        for k in zorder + [0]:
            dst = lax.rem(z + k, nz)
            for q in both:
                @pl.when(dst > z if k else core != q)
                def _():
                    remote(
                        fs_src.at[u, q, dst], fs_dst.at[u, core, z],
                        fs_ss.at[u, q, k], fs_rs.at[u, core, z], (chip * 2 + q, dst),
                    ).start()

    def fs_finish(u):
        arrived("fs", u)
        res = []
        for h in both:
            acc = jnp.where(core == h, fs_src[u, h, z], fs_dst[u, h, nz - 1])
            for j in range(nz - 1):
                acc = acc + fs_dst[u, h, j]
            res.append(jnp.concatenate([acc, turn(acc, 2)], axis=0))
        return res

    def write(lev, x0, x1):
        out[lev, 0] = jnp.where(low, x0, pltpu.roll(x1, HALF, 1))
        out[lev, 1] = jnp.where(low, pltpu.roll(x0, HALF, 1), x1)

    def chunks(lev, p, n):
        return ag.at[lev, p, pl.ds(0, n * CH)]

    def ag_first(s, val):
        def arrive():
            @pl.when(core == s)
            def _():
                wait_bytes(chunks(0, s, nz - 1), ag_rs.at[0, s])

            @pl.when(core != s)
            def _():
                wait_bytes(chunks(0, s, nz), ag_rs.at[0, s])

        def left():
            wait_bytes(chunks(0, s, nz - 1), ag_ss.at[0, s])

            @pl.when(core != s)
            def _():
                wait_bytes(av.at[s], sib_ss.at[AV])

        due["ag", 0, s] = arrive
        sent.append(left)
        av[s] = val
        dst = ag.at[0, core, mine]
        for k in zorder:
            remote(
                av.at[s], dst, ag_ss.at[0, s], ag_rs.at[0, core], (chip * 2 + s, lax.rem(z + k, nz))
            ).start()

        @pl.when(core != s)
        def _():
            remote(av.at[s], dst, sib_ss.at[AV], ag_rs.at[0, core], sibling).start()

        @pl.when(core == s)
        def _():
            ag[0, core, mine] = val

    def ag_send(lev, p, val):
        others = chunks(lev, p, nz - 1)
        due["ag", lev, p] = lambda: wait_bytes(others, ag_rs.at[lev, p])
        sent.append(lambda: wait_bytes(others, ag_ss.at[lev, p]))
        ag[lev, p, mine] = val
        part = ag.at[lev, p, mine]
        for k in zorder:
            remote(part, part, ag_ss.at[lev, p], ag_rs.at[lev, p], zpeer(k)).start()

    relays = {
        8: [
            [(0, 1, None), (0, -1, None)],
            [(-1, 1, None), (1, -1, None)],
            [(-2, 2, 0), (2, -2, 1), (-2, 1, None), (2, -1, None)],
        ],
        4: [[(0, 1, None), (0, -1, None)], [(-1, 1, 0), (1, -1, 1)]],
    }[nz]

    def dg_copies(lev, step):
        d = lev - 1
        res = []
        for i, (off, far, n) in enumerate(relays[step]):
            rows = pl.ds(lax.rem(z + off + nz, nz) * CH, CH)
            part = dg.at[d, :, rows] if n is None else dg.at[d, n, rows]
            res.append(remote(part, part, dg_ss.at[d, step, i], dg_rs.at[d, step, i], zpeer(far + nz)))
        return res

    def dg_step(lev, step):
        if step >= len(relays) or lev > 2:
            return
        if step > 0:
            arrived("dg", lev, step - 1)
        else:
            dg[lev - 1, :, mine] = dinv_v[lev]
        copies = dg_copies(lev, step)
        due["dg", lev, step] = lambda: [c.wait_recv() for c in copies]
        sent.append(lambda: [c.wait_send() for c in copies])
        for c in copies:
            c.start()

    def dg_finish(lev):
        arrived("dg", lev, len(relays) - 1)
        for n in both:
            dgt[lev - 1, core, n] = jnp.transpose(dg[lev - 1, n])
        sib_send(DGT + lev, dgt.at[lev - 1, core], dgt.at[lev - 1, core])

    def combine_panels(lev):
        arrived("pan", lev)
        for n in both:
            weight = {}
            for a in range(KB):
                for b in range(a + 1, KB):
                    same = tgt[lev, n, a] == tgt[lev, n, b]
                    weight[a, b] = jnp.where(same, 1.0, 0.0)

            def step(i, _, n=n, weight=weight):
                rows = pl.ds(pl.multiple_of(i * 8, 8), 8)
                vals = [pan_v[lev, core, n, k, rows] for k in range(KB)]
                for a in range(KB):
                    acc = vals[a]
                    for b in range(KB):
                        if b != a:
                            acc = acc + weight[min(a, b), max(a, b)] * vals[b]
                    pan_v[lev, core, n, a, rows] = acc
                return 0

            lax.fori_loop(0, CH // 8, step, 0)
        sib_send(PAN + lev, pan_v.at[lev, core], pan_v.at[lev, core])

    def gather(lev, level_to, u, b):
        t = level_to * count + b * 4
        e = []
        for j in range(4):
            acc = None
            for m in range(4):
                block = dbuf[lev, u, m, tbl_s[m // 2, 2 * lev + m % 2, t + j]]
                acc = block if m == 0 else acc + block
            e.append(acc)
        return quarters(*e)

    def spread(lev, level_to, p):
        group = min(chips, 4)

        def step(i, _):
            vals = []
            for j in range(group):
                b = i * group + j
                val = gather(lev, level_to, p, b)
                if lev > 0:
                    val = val + dense[level_to - 1, p, b]
                vals.append(val)
            for j, val in enumerate(vals):
                dense[level_to - 1, p, i * group + j] = val
            return 0

        lax.fori_loop(0, chips // group, step, 0, unroll=True)

    def solve(lev, u, a):
        if lev > 0:
            arrived("ag", lev, u)
            r = ag[lev, u]
            a = quarters(*[dot(dgt[lev - 1, m // 2, m % 2], r) for m in range(4)])
            tmp[...] = a
            yv[lev - 1, u] = tmp[mine]
        turned = [turn(a, k) for k in range(4)]
        for m in range(4):
            am = quarters(*[turned[(j - m) % 4] for j in range(4)])
            d = dot(pan_v[lev, m // 2, m % 2].reshape(KB * CH, width), am)
            dbuf[lev, u, m, pl.ds(0, KB)] = d.reshape(KB, CH, LANES)

    def xy_send(lev, p):
        due["xy", lev, p] = lambda: wait_bytes(xy.at[lev, p], xy_rs.at[lev, p])
        sent.append(lambda: wait_bytes(xy.at[lev, p], xy_ss.at[lev, p]))
        for i, (dx, dy) in enumerate(offsets):
            peer, dev = xypeer(dx, dy)
            remote(dense.at[lev, p, peer], xy.at[lev, p, i], xy_ss.at[lev, p], xy_rs.at[lev, p], dev).start()

    def residual(lev, p):
        arrived("xy", lev, p)
        acc = dense[lev, p, chip]
        for i in range(len(offsets)):
            acc = acc + xy[lev, p, i]
        return rq[p, lev] - acc

    pl.semaphore_wait(barrier, 2 * (nz - 1) + len(offsets) + 1)

    for s in both:
        rs_send(s)
    sib_send(TBL, tbl_v.at[core], tbl_v.at[core])
    sib_send(RHS, rp.at[1 - core, pl.ds(1, LEVELS - 1)], rqp.at[core])
    sib_send(INV, dinv_v.at[LEVELS - 1], dinv_x.at[core])
    rqp[core] = rp[core, pl.ds(1, LEVELS - 1)]
    dinv_x[core] = dinv_v[LEVELS - 1]
    dg_step(1, 0)
    combine_panels(0)
    first = []
    for s in both:
        val = rs_finish(s)
        ag_first(s, val)
        first.append(val)
    dg_step(1, 1)
    write(0, *first)
    arrived("sib", TBL)
    c_tbl = pltpu.make_async_copy(tbl_v, tbl_s, loc.at[5])
    c_tbl.start()
    due["tbl",] = c_tbl.wait
    combine_panels(1)
    combine_panels(2)
    arrived("tbl")
    arrived("sib", RHS)
    arrived("sib", INV)
    for lev in range(LEVELS - 1):
        rq[0, lev], rq[1, lev] = to_streams(rqp[0, lev], rqp[1, lev])
    for lev in range(LEVELS - 1):
        arrived("sib", PAN + lev)
        if lev > 0:
            arrived("sib", DGT + lev)
        if lev == 0:
            arrived("ag", 0, 0)
            arrived("ag", 0, 1)
            start = to_streams(ag[0, 0], ag[0, 1])
        for u in both:
            solve(lev, u, start[u])
            spread(lev, lev + 1, u)
            xy_send(lev, u)
        dg_step(lev + 1, 2)
        dg_step(lev + 2, 0)
        if lev > 0:
            packs = to_packs(yv[lev - 1, 0], yv[lev - 1, 1])
            yo[lev - 1, 0] = jnp.where(core == 0, packs[0], packs[1])
            yo[lev - 1, 1] = jnp.where(core == 0, packs[1], packs[0])
            sib_send(ANS + lev, yo.at[lev - 1, 1], yx.at[lev - 1])
        for to in range(lev + 2, LEVELS):
            for p in both:
                spread(lev, to, p)
        if lev < LEVELS - 2:
            for p in both:
                ag_send(lev + 1, p, residual(lev, p))
            dg_finish(lev + 1)
            dg_step(lev + 2, 1)
        else:
            for p in both:
                fs_send(p, residual(lev, p))
    for lev in (1, 2):
        arrived("sib", ANS + lev)
        own, other = yo[lev - 1, 0], yx[lev - 1]
        write(lev, jnp.where(core == 0, own, other), jnp.where(core == 0, other, own))
    for wait in sent:
        wait()
    last = [fs_finish(0), fs_finish(1)]
    write(LEVELS - 1, *[
        quarters(last[0][h], turn(last[1][h], 1), turn(last[0][h], 1), turn(last[1][h], 2)) for h in both
    ])


TBL, RHS, INV, AV, PAN, DGT, ANS, SIBS = 0, 1, 2, 3, 4, 6, 8, 11


def shards(nx, ny, nz, right_side, diag_inverse, panels, targets):
    chips = nx * ny
    width = CH * nz
    count = 4 * chips
    f32 = jnp.float32
    dma = pltpu.SemaphoreType.DMA
    vmem = pltpu.VMEM
    solved = LEVELS - 1
    hbm = pl.BlockSpec(memory_space=pltpu.HBM)
    return pl.pallas_call(
        functools.partial(kernel, nx, ny, nz),
        out_shape=jax.ShapeDtypeStruct((LEVELS, 2, CH, LANES), f32),
        in_specs=[hbm] * 4,
        out_specs=pl.BlockSpec(memory_space=pltpu.VMEM),
        scratch_shapes=[
            pltpu.SMEM((solved, 2, KB), jnp.int32),
            vmem((LEVELS, 2, CH, LANES), f32),
            vmem((LEVELS, 2, CH, width), f32),
            vmem((2, 2, CH, width), f32),
            vmem((solved, 2, 2, KB, CH, width), f32),
            vmem((2, 8, LEVELS * count), jnp.int32),
            pltpu.SMEM((2, 8, LEVELS * count), jnp.int32),
            vmem((2, LEVELS, CH, LANES), f32),
            vmem((2, solved, CH, LANES), f32),
            vmem((2, solved, CH, LANES), f32),
            vmem((2, width, LANES), f32),
            vmem((2, nz, CH, LANES), f32),
            vmem((2, 2, nz, CH // 2, LANES), f32),
            vmem((2, 2, nz, CH // 2, LANES), f32),
            vmem((2, CH, LANES), f32),
            vmem((solved, 2, width, LANES), f32),
            vmem((2, 2, width, width), f32),
            vmem((2, 2, 2, width, width), f32),
            vmem((solved, 2, 4, KB + 1, CH, LANES), f32),
            vmem((solved, 2, chips, CH, LANES), f32),
            vmem((solved, 2, chips - 1, CH, LANES), f32),
            vmem((width, LANES), f32),
            vmem((2, 2, CH, LANES), f32),
            vmem((2, 2, CH, LANES), f32),
            vmem((2, CH, LANES), f32),
            dma((7,)),
            dma((2, nz)),
            dma((2, nz)),
            dma((2, 2, nz)),
            dma((2, 2, nz)),
            dma((solved, 2)),
            dma((solved, 2)),
            dma((2, 3, 4)),
            dma((2, 3, 4)),
            dma((solved, 2)),
            dma((solved, 2)),
            dma((SIBS,)),
            dma((SIBS,)),
        ],
        compiler_params=pltpu.CompilerParams(
            collective_id=0, has_side_effects=True, vmem_limit_bytes=60 * 1024 * 1024
        ),
    )(right_side, jnp.swapaxes(diag_inverse, 2, 3), panels, targets)


def solution(mesh):
    prow, nz = mesh.shape["prow"], mesh.shape["pcol"]
    ny = 4 if prow == 32 else 1
    nx = prow // (2 * ny)
    in_specs = (
        P(None, "prow", "pcol", None),
        P(None, "prow", None, "pcol"),
        P(None, "prow", None, "pcol", None),
        P(None, "prow", None),
    )
    return jax.shard_map(
        functools.partial(shards, nx, ny, nz), mesh=mesh, in_specs=in_specs,
        out_specs=P(None, "prow", "pcol", None), check_vma=False,
    )
```

```python
import functools

import jax
import jax.numpy as jnp
from jax import lax
from jax.experimental import pallas as pl
from jax.experimental.pallas import tpu as pltpu
from jax.sharding import PartitionSpec as P

MESH = pl.DeviceIdType.MESH
LEVELS = 4
CH = 32
LANES = 128
HALF = 64
KB = 8


def split(a):
    hi = a.astype(jnp.bfloat16)
    return hi, (a - hi.astype(jnp.float32)).astype(jnp.bfloat16)


def dot3(a, b, dims):
    ah, al = split(a)
    bh, bl = split(b)
    f = functools.partial(
        lax.dot_general, dimension_numbers=(dims, ((), ())), preferred_element_type=jnp.float32
    )
    n = b.shape[1]
    wide = f(ah, jnp.concatenate([bh, bl], axis=1))
    return wide[:, :n] + (wide[:, n:] + f(al, bh))


def dot(a, b):
    return dot3(a, b, ((1,), (0,)))


def dot_t(a, b):
    return dot3(a, b, ((0,), (0,)))


def kernel(
    nx, ny, nz,
    rhs_hbm, dinv_hbm, pan_hbm, tgt_hbm, out,
    tgt, rhs_v, dinv_v, dinv_x, pan_v, tbl_v, tbl_s, rp, rqp, rq, rs_src, rs_dst, fs_src, fs_dst, av, ag, dg, dgt,
    dbuf, dense, xy, tmp, yv, yo, yx,
    loc, rs_ss, rs_rs, fs_ss, fs_rs, ag_ss, ag_rs, dg_ss, dg_rs, xy_ss, xy_rs, sib_ss, sib_rs,
):
    chips = nx * ny
    width = CH * nz
    count = 4 * chips
    prow = lax.axis_index("prow")
    z = lax.axis_index("pcol")
    core = lax.rem(prow, 2)
    chip = prow // 2
    x = chip // ny
    y = lax.rem(chip, ny)
    both = range(2)
    mine = pl.ds(z * CH, CH)

    def zpeer(k):
        return prow, lax.rem(z + k, nz)

    def xypeer(dx, dy):
        peer = lax.rem(x + dx, nx) * ny + lax.rem(y + dy, ny)
        return peer, (peer * 2 + core, z)

    sibling = (chip * 2 + 1 - core, z)
    offsets = [(dx, dy) for dx in range(nx) for dy in range(ny) if dx or dy]
    offsets.sort(key=lambda o: -(min(o[0], nx - o[0]) + min(o[1], ny - o[1])))
    zorder = sorted(range(1, nz), key=lambda k: -min(k, nz - k))

    def remote(src, dst, ss, rs, dev):
        return pltpu.make_async_remote_copy(
            src_ref=src, dst_ref=dst, send_sem=ss, recv_sem=rs, device_id=dev, device_id_type=MESH
        )

    due, sent = {}, []

    def arrived(*name):
        due.pop(name)()

    def wait_bytes(ref, sem):
        pltpu.make_async_copy(ref, ref, sem).wait()

    c_rhs = pltpu.make_async_copy(rhs_hbm, rhs_v, loc.at[0])
    c_dinv = pltpu.make_async_copy(dinv_hbm, dinv_v, loc.at[1])
    c_tgt = pltpu.make_async_copy(tgt_hbm, tgt, loc.at[6])
    c_tgt.start()
    c_rhs.start()
    c_dinv.start()
    for lev in range(LEVELS - 1):
        c = pltpu.make_async_copy(pan_hbm.at[lev], pan_v.at[lev, core], loc.at[2 + lev])
        c.start()
        due["pan", lev] = c.wait

    barrier = pltpu.get_barrier_semaphore()
    for k in zorder:
        for c in both:
            pl.semaphore_signal(
                barrier, inc=1, device_id=(chip * 2 + c, lax.rem(z + k, nz)), device_id_type=MESH
            )
    for dx, dy in offsets:
        pl.semaphore_signal(barrier, inc=1, device_id=xypeer(dx, dy)[1], device_id_type=MESH)
    pl.semaphore_signal(barrier, inc=1, device_id=sibling, device_id_type=MESH)

    lane = lax.broadcasted_iota(jnp.int32, (1, LANES), 1)
    low = lane < HALF
    first_q, third_q = lane < HALF // 2, lane < HALF // 2 * 3

    def quarters(a, b, c, d):
        return jnp.where(low, jnp.where(first_q, a, b), jnp.where(third_q, c, d))

    def turn(v, k):
        return pltpu.roll(v, k % 4 * (HALF // 2), 1) if k % 4 else v

    def to_streams(v, w):
        return (
            quarters(v, turn(v, -1), turn(w, 2), turn(w, 1)),
            quarters(turn(v, -1), turn(v, -2), turn(w, 1), w),
        )

    def to_packs(v, w):
        return (
            quarters(v, turn(w, 1), turn(v, 1), turn(w, 2)),
            quarters(turn(v, -2), turn(w, -1), turn(v, -1), w),
        )

    def sib_send(i, src, dst):
        c = remote(src, dst, sib_ss.at[i], sib_rs.at[i], sibling)
        c.start()
        due["sib", i] = c.wait_recv
        sent.append(c.wait_send)

    c_rhs.wait()
    for lev in range(LEVELS):
        r0, r1 = rhs_v[lev, 0], rhs_v[lev, 1]
        rp[0, lev] = jnp.where(low, r0, pltpu.roll(r1, HALF, 1))
        rp[1, lev] = jnp.where(low, pltpu.roll(r0, HALF, 1), r1)
    c_dinv.wait()
    for s in both:
        r = rp[s, 0]
        rs_src[s] = jnp.where(low, dot_t(dinv_v[0, 0], r), dot_t(dinv_v[0, 1], r))

    c_tgt.wait()
    ids = lax.broadcasted_iota(jnp.int32, (1, LEVELS * count), 1)
    for row in range(8):
        found = jnp.full((1, LEVELS * count), KB, jnp.int32)
        if row < 2 * (LEVELS - 1):
            for k in reversed(range(KB)):
                found = jnp.where(ids == tgt[row // 2, row % 2, k], k, found)
        tbl_v[core, pl.ds(row, 1), :] = found

    for lev in range(LEVELS - 1):
        for u in both:
            for m in range(4):
                dbuf[lev, u, m, KB] = jnp.zeros((CH, LANES), jnp.float32)
    for s in both:
        for j in range(nz):
            @pl.when(j >= z)
            def _():
                rs_dst[s, j] = jnp.zeros((CH, LANES), jnp.float32)

            @pl.when((j > z) | ((j == z) & (core == s)))
            def _():
                for u in both:
                    fs_dst[u, s, j] = jnp.zeros((CH // 2, LANES), jnp.float32)

    def rs_send(s):
        def arrive():
            for j in range(nz - 1):
                @pl.when(j < z)
                def _():
                    wait_bytes(rs_dst.at[s, j], rs_rs.at[s, j])

        def left():
            for k in range(1, nz):
                @pl.when(lax.rem(z + k, nz) > z)
                def _():
                    wait_bytes(rs_src.at[s, pl.ds(0, CH)], rs_ss.at[s, k])

        due["rs", s] = arrive
        sent.append(left)
        for k in zorder:
            dst = lax.rem(z + k, nz)

            @pl.when(dst > z)
            def _():
                remote(
                    rs_src.at[s, pl.ds(dst * CH, CH)], rs_dst.at[s, z],
                    rs_ss.at[s, k], rs_rs.at[s, z], (prow, dst),
                ).start()

    def rs_finish(s):
        arrived("rs", s)
        acc = rs_src[s, mine]
        for j in range(nz - 1):
            acc = acc + rs_dst[s, j]
        return acc

    def fs_send(u, r):
        p = quarters(*[dot_t(dinv_x[m // 2, m % 2], r) for m in range(4)])
        for b in range(nz):
            top, bottom = p[b * CH : b * CH + CH // 2], p[b * CH + CH // 2 : (b + 1) * CH]
            fs_src[u, 0, b] = jnp.where(low, top, turn(bottom, 2))
            fs_src[u, 1, b] = jnp.where(low, turn(top, 2), bottom)

        def arrive():
            for h in both:
                for j in range(nz):
                    @pl.when((j < z) | ((j == z) & (core != h)))
                    def _():
                        wait_bytes(fs_dst.at[u, h, j], fs_rs.at[u, h, j])

        def left():
            for q in both:
                for k in range(nz):
                    @pl.when(lax.rem(z + k, nz) > z if k else core != q)
                    def _():
                        wait_bytes(fs_src.at[u, q, 0], fs_ss.at[u, q, k])

        due["fs", u] = arrive
        sent.append(left)
        for k in zorder + [0]:
            dst = lax.rem(z + k, nz)
            for q in both:
                @pl.when(dst > z if k else core != q)
                def _():
                    remote(
                        fs_src.at[u, q, dst], fs_dst.at[u, core, z],
                        fs_ss.at[u, q, k], fs_rs.at[u, core, z], (chip * 2 + q, dst),
                    ).start()

    def fs_finish(u):
        arrived("fs", u)
        res = []
        for h in both:
            acc = jnp.where(core == h, fs_src[u, h, z], fs_dst[u, h, nz - 1])
            for j in range(nz - 1):
                acc = acc + fs_dst[u, h, j]
            res.append(jnp.concatenate([acc, turn(acc, 2)], axis=0))
        return res

    def write(lev, x0, x1):
        out[lev, 0] = jnp.where(low, x0, pltpu.roll(x1, HALF, 1))
        out[lev, 1] = jnp.where(low, pltpu.roll(x0, HALF, 1), x1)

    def chunks(lev, p, n):
        return ag.at[lev, p, pl.ds(0, n * CH)]

    def ag_first(s, val):
        def arrive():
            @pl.when(core == s)
            def _():
                wait_bytes(chunks(0, s, nz - 1), ag_rs.at[0, s])

            @pl.when(core != s)
            def _():
                wait_bytes(chunks(0, s, nz), ag_rs.at[0, s])

        def left():
            wait_bytes(chunks(0, s, nz - 1), ag_ss.at[0, s])

            @pl.when(core != s)
            def _():
                wait_bytes(av.at[s], sib_ss.at[AV])

        due["ag", 0, s] = arrive
        sent.append(left)
        av[s] = val
        dst = ag.at[0, core, mine]
        for k in zorder:
            remote(
                av.at[s], dst, ag_ss.at[0, s], ag_rs.at[0, core], (chip * 2 + s, lax.rem(z + k, nz))
            ).start()

        @pl.when(core != s)
        def _():
            remote(av.at[s], dst, sib_ss.at[AV], ag_rs.at[0, core], sibling).start()

        @pl.when(core == s)
        def _():
            ag[0, core, mine] = val

    def ag_send(lev, p, val):
        others = chunks(lev, p, nz - 1)
        due["ag", lev, p] = lambda: wait_bytes(others, ag_rs.at[lev, p])
        sent.append(lambda: wait_bytes(others, ag_ss.at[lev, p]))
        ag[lev, p, mine] = val
        part = ag.at[lev, p, mine]
        for k in zorder:
            remote(part, part, ag_ss.at[lev, p], ag_rs.at[lev, p], zpeer(k)).start()

    relays = {
        8: [
            [(0, 1, None), (0, -1, None)],
            [(-1, 1, None), (1, -1, None)],
            [(-2, 2, 0), (2, -2, 1), (-2, 1, None), (2, -1, None)],
        ],
        4: [[(0, 1, None), (0, -1, None)], [(-1, 1, 0), (1, -1, 1)]],
    }[nz]

    def dg_copies(lev, step):
        d = lev - 1
        res = []
        for i, (off, far, n) in enumerate(relays[step]):
            rows = pl.ds(lax.rem(z + off + nz, nz) * CH, CH)
            part = dg.at[d, :, rows] if n is None else dg.at[d, n, rows]
            res.append(remote(part, part, dg_ss.at[d, step, i], dg_rs.at[d, step, i], zpeer(far + nz)))
        return res

    def dg_step(lev, step):
        if step >= len(relays) or lev > 2:
            return
        if step > 0:
            arrived("dg", lev, step - 1)
        else:
            dg[lev - 1, :, mine] = dinv_v[lev]
        copies = dg_copies(lev, step)
        due["dg", lev, step] = lambda: [c.wait_recv() for c in copies]
        sent.append(lambda: [c.wait_send() for c in copies])
        for c in copies:
            c.start()

    def dg_finish(lev):
        arrived("dg", lev, len(relays) - 1)
        for n in both:
            dgt[lev - 1, core, n] = jnp.transpose(dg[lev - 1, n])
        sib_send(DGT + lev, dgt.at[lev - 1, core], dgt.at[lev - 1, core])

    def combine_panels(lev):
        arrived("pan", lev)
        for n in both:
            weight = {}
            for a in range(KB):
                for b in range(a + 1, KB):
                    same = tgt[lev, n, a] == tgt[lev, n, b]
                    weight[a, b] = jnp.where(same, 1.0, 0.0)

            def step(i, _, n=n, weight=weight):
                rows = pl.ds(pl.multiple_of(i * 8, 8), 8)
                vals = [pan_v[lev, core, n, k, rows] for k in range(KB)]
                for a in range(KB):
                    acc = vals[a]
                    for b in range(KB):
                        if b != a:
                            acc = acc + weight[min(a, b), max(a, b)] * vals[b]
                    pan_v[lev, core, n, a, rows] = acc
                return 0

            lax.fori_loop(0, CH // 8, step, 0)
        sib_send(PAN + lev, pan_v.at[lev, core], pan_v.at[lev, core])

    def gather(lev, level_to, u, b):
        t = level_to * count + b * 4
        e = []
        for j in range(4):
            acc = None
            for m in range(4):
                block = dbuf[lev, u, m, tbl_s[m // 2, 2 * lev + m % 2, t + j]]
                acc = block if m == 0 else acc + block
            e.append(acc)
        return quarters(*e)

    def spread(lev, level_to, p):
        group = min(chips, 4)

        def step(i, _):
            vals = []
            for j in range(group):
                b = i * group + j
                val = gather(lev, level_to, p, b)
                if lev > 0:
                    val = val + dense[level_to - 1, p, b]
                vals.append(val)
            for j, val in enumerate(vals):
                dense[level_to - 1, p, i * group + j] = val
            return 0

        lax.fori_loop(0, chips // group, step, 0, unroll=True)

    def solve(lev, u, a):
        if lev > 0:
            arrived("ag", lev, u)
            r = ag[lev, u]
            a = quarters(*[dot(dgt[lev - 1, m // 2, m % 2], r) for m in range(4)])
            tmp[...] = a
            yv[lev - 1, u] = tmp[mine]
        turned = [turn(a, k) for k in range(4)]
        for m in range(4):
            am = quarters(*[turned[(j - m) % 4] for j in range(4)])
            d = dot(pan_v[lev, m // 2, m % 2].reshape(KB * CH, width), am)
            dbuf[lev, u, m, pl.ds(0, KB)] = d.reshape(KB, CH, LANES)

    def xy_send(lev, p):
        due["xy", lev, p] = lambda: wait_bytes(xy.at[lev, p], xy_rs.at[lev, p])
        sent.append(lambda: wait_bytes(xy.at[lev, p], xy_ss.at[lev, p]))
        for i, (dx, dy) in enumerate(offsets):
            peer, dev = xypeer(dx, dy)
            remote(dense.at[lev, p, peer], xy.at[lev, p, i], xy_ss.at[lev, p], xy_rs.at[lev, p], dev).start()

    def residual(lev, p):
        arrived("xy", lev, p)
        acc = dense[lev, p, chip]
        for i in range(len(offsets)):
            acc = acc + xy[lev, p, i]
        return rq[p, lev] - acc

    pl.semaphore_wait(barrier, 2 * (nz - 1) + len(offsets) + 1)

    for s in both:
        rs_send(s)
    sib_send(TBL, tbl_v.at[core], tbl_v.at[core])
    sib_send(RHS, rp.at[1 - core, pl.ds(1, LEVELS - 1)], rqp.at[core])
    sib_send(INV, dinv_v.at[LEVELS - 1], dinv_x.at[core])
    rqp[core] = rp[core, pl.ds(1, LEVELS - 1)]
    dinv_x[core] = dinv_v[LEVELS - 1]
    dg_step(1, 0)
    combine_panels(0)
    first = []
    for s in both:
        val = rs_finish(s)
        ag_first(s, val)
        first.append(val)
    dg_step(1, 1)
    write(0, *first)
    arrived("sib", TBL)
    c_tbl = pltpu.make_async_copy(tbl_v, tbl_s, loc.at[5])
    c_tbl.start()
    due["tbl",] = c_tbl.wait
    combine_panels(1)
    combine_panels(2)
    arrived("tbl")
    arrived("sib", RHS)
    arrived("sib", INV)
    for lev in range(LEVELS - 1):
        rq[0, lev], rq[1, lev] = to_streams(rqp[0, lev], rqp[1, lev])
    for lev in range(LEVELS - 1):
        arrived("sib", PAN + lev)
        if lev > 0:
            arrived("sib", DGT + lev)
        if lev == 0:
            arrived("ag", 0, 0)
            arrived("ag", 0, 1)
            start = to_streams(ag[0, 0], ag[0, 1])
        for u in both:
            solve(lev, u, start[u])
            spread(lev, lev + 1, u)
            xy_send(lev, u)
        dg_step(lev + 1, 2)
        dg_step(lev + 2, 0)
        if lev > 0:
            packs = to_packs(yv[lev - 1, 0], yv[lev - 1, 1])
            yo[lev - 1, 0] = jnp.where(core == 0, packs[0], packs[1])
            yo[lev - 1, 1] = jnp.where(core == 0, packs[1], packs[0])
            sib_send(ANS + lev, yo.at[lev - 1, 1], yx.at[lev - 1])
        if lev + 2 < LEVELS:
            for p in both:
                spread(lev, lev + 2, p)
        if lev < LEVELS - 2:
            for p in both:
                ag_send(lev + 1, p, residual(lev, p))
            dg_finish(lev + 1)
            dg_step(lev + 2, 1)
            for to in range(lev + 3, LEVELS):
                for p in both:
                    spread(lev, to, p)
        else:
            for p in both:
                fs_send(p, residual(lev, p))
    for lev in (1, 2):
        arrived("sib", ANS + lev)
        own, other = yo[lev - 1, 0], yx[lev - 1]
        write(lev, jnp.where(core == 0, own, other), jnp.where(core == 0, other, own))
    for wait in sent:
        wait()
    last = [fs_finish(0), fs_finish(1)]
    write(LEVELS - 1, *[
        quarters(last[0][h], turn(last[1][h], 1), turn(last[0][h], 1), turn(last[1][h], 2)) for h in both
    ])


TBL, RHS, INV, AV, PAN, DGT, ANS, SIBS = 0, 1, 2, 3, 4, 6, 8, 11


def shards(nx, ny, nz, right_side, diag_inverse, panels, targets):
    chips = nx * ny
    width = CH * nz
    count = 4 * chips
    f32 = jnp.float32
    dma = pltpu.SemaphoreType.DMA
    vmem = pltpu.VMEM
    solved = LEVELS - 1
    hbm = pl.BlockSpec(memory_space=pltpu.HBM)
    return pl.pallas_call(
        functools.partial(kernel, nx, ny, nz),
        out_shape=jax.ShapeDtypeStruct((LEVELS, 2, CH, LANES), f32),
        in_specs=[hbm] * 4,
        out_specs=pl.BlockSpec(memory_space=pltpu.VMEM),
        scratch_shapes=[
            pltpu.SMEM((solved, 2, KB), jnp.int32),
            vmem((LEVELS, 2, CH, LANES), f32),
            vmem((LEVELS, 2, CH, width), f32),
            vmem((2, 2, CH, width), f32),
            vmem((solved, 2, 2, KB, CH, width), f32),
            vmem((2, 8, LEVELS * count), jnp.int32),
            pltpu.SMEM((2, 8, LEVELS * count), jnp.int32),
            vmem((2, LEVELS, CH, LANES), f32),
            vmem((2, solved, CH, LANES), f32),
            vmem((2, solved, CH, LANES), f32),
            vmem((2, width, LANES), f32),
            vmem((2, nz, CH, LANES), f32),
            vmem((2, 2, nz, CH // 2, LANES), f32),
            vmem((2, 2, nz, CH // 2, LANES), f32),
            vmem((2, CH, LANES), f32),
            vmem((solved, 2, width, LANES), f32),
            vmem((2, 2, width, width), f32),
            vmem((2, 2, 2, width, width), f32),
            vmem((solved, 2, 4, KB + 1, CH, LANES), f32),
            vmem((solved, 2, chips, CH, LANES), f32),
            vmem((solved, 2, chips - 1, CH, LANES), f32),
            vmem((width, LANES), f32),
            vmem((2, 2, CH, LANES), f32),
            vmem((2, 2, CH, LANES), f32),
            vmem((2, CH, LANES), f32),
            dma((7,)),
            dma((2, nz)),
            dma((2, nz)),
            dma((2, 2, nz)),
            dma((2, 2, nz)),
            dma((solved, 2)),
            dma((solved, 2)),
            dma((2, 3, 4)),
            dma((2, 3, 4)),
            dma((solved, 2)),
            dma((solved, 2)),
            dma((SIBS,)),
            dma((SIBS,)),
        ],
        compiler_params=pltpu.CompilerParams(
            collective_id=0, has_side_effects=True, vmem_limit_bytes=60 * 1024 * 1024
        ),
    )(right_side, jnp.swapaxes(diag_inverse, 2, 3), panels, targets)


def solution(mesh):
    prow, nz = mesh.shape["prow"], mesh.shape["pcol"]
    ny = 4 if prow == 32 else 1
    nx = prow // (2 * ny)
    in_specs = (
        P(None, "prow", "pcol", None),
        P(None, "prow", None, "pcol"),
        P(None, "prow", None, "pcol", None),
        P(None, "prow", None),
    )
    return jax.shard_map(
        functools.partial(shards, nx, ny, nz), mesh=mesh, in_specs=in_specs,
        out_specs=P(None, "prow", "pcol", None), check_vma=False,
    )
```
